32 devices in a mesh: groups: 2 (over y), freq: 16 (over z, x, core).
Axes of the slice: x: 2, y: 2, z: 4, core: 2. Of those that a mesh axis runs over, the one named last changes fastest.
Arguments:
- signal: float32 [1024, 8, 4096], P('freq', None, 'groups'), parts along dimension 2, may hold values from -6 to 6
- offsets: int32 [8], replicated, may hold values from 0 to 4095
- pairing: int32 [4096], P('groups'), parts along dimension 0, may hold values from 0 to 2047, each once
- modes_kept: int32 [512], replicated, may hold values from 1 to 4, as said below
Outputs:
- energy: float32 [512, 8], P('freq', 'groups'), parts along dimension 1
- modes: float32 [512, 4, 2, 2, 2048], P(None, None, None, None, ('groups', 'freq')), parts along dimension 4
The draws below stay inside these ranges and needn't reach their ends.
There are 2 independent parts, one for each index of `groups`. The reference program is written for one: setup_inputs(seed, part) draws one part's arguments, and reference() takes and returns one part's arrays. A program takes and returns all parts, laid end to end along the dimension named above; an argument that names none is the same for every part. Nothing has to cross between parts.
Inputs may be any that keep to these rules, and one draw needn't show every extreme that they name: `modes_kept`: every value from 1 to 4 occurs. `pairing`: a permutation of the 2048 points.
All inputs are finite; a program needn't handle non-finite values.
Results may differ from the reference program's by a relative error of at most 0.0001.
Values sent between devices are 32-bit elements; how exact they have to be, the bound alone decides.
No kernel may reach another device: no remote copies, remote signals or barrier semaphores. Data moves between devices by JAX's collectives and lax.ppermute only.
A program may use at most 128 MiB of HBM per device.

```python
import math
import jax
import jax.numpy as jnp
from jax import lax

NF = 1024
KB = 512
NB = 8
P_SIZE = 2048
NPAIR = 1024
M = 4
ITERS = 3


def draw_modes_kept(key, part):
    key_values, key_low, key_high = jax.random.split(key, 3)
    values = jax.random.randint(key_values, (KB,), 1, M + 1)
    low_spot = jax.random.randint(key_low, (), 0, KB // 2)
    high_spot = jax.random.randint(key_high, (), KB // 2, KB)
    values = values.at[low_spot].set(1).at[high_spot].set(M)
    return values.astype(jnp.int32)


def with_ends(entries, stream_key, least, top_value):
    spot = [jax.random.randint(jax.random.fold_in(stream_key, axis), (), 0, length) for axis, length in enumerate(entries.shape)]
    longest = entries.shape.index(max(entries.shape))
    neighbour = spot[:longest] + [(spot[longest] + 1) % entries.shape[longest]] + spot[longest + 1:]
    return entries.at[tuple(spot)].set(least).at[tuple(neighbour)].set(top_value)


def block_levels(own_key, dims, cuts, least, largest):
    gain, own = 1.0, jax.random.fold_in(own_key, 6)
    for axis_at, parts in cuts:
        heights = jnp.exp(jax.random.uniform(jax.random.fold_in(own, axis_at), (parts,), jnp.float32, least / len(cuts), largest / len(cuts)))
        gain = gain * jnp.repeat(heights, dims[axis_at] // parts).reshape([-1 if axis == axis_at else 1 for axis in range(len(dims))])
    return gain


def bell_draw(rng, dims, scale, bound, cuts=(), kind=jnp.bfloat16):
    result = jax.random.normal(rng, dims, jnp.float32) * scale
    if len(cuts) > 0:
        result = block_levels(rng, dims, cuts, -0.22, 0.18) * result
    return jnp.clip(result, min=-bound, max=bound).astype(kind)


def setup_inputs(seed: int = 0, part: int = 0) -> dict:
    streams_of = jax.random.split(jax.random.key(seed), 5)
    part_splits = jax.random.split(jax.random.fold_in(streams_of[4], part), 5)
    return {
        "signal": bell_draw(part_splits[0], (NF, NB, P_SIZE), 1.0, 6.0, ((0, 16),), jnp.float32),
        "offsets": with_ends(jax.random.randint(streams_of[1], (NB,), 0, NB * NF // 2), jax.random.fold_in(streams_of[1], 1), 0, (NB * NF // 2) - 1).astype(jnp.int32),
        "pairing": jax.random.permutation(part_splits[2], P_SIZE).astype(jnp.int32),
        "modes_kept": draw_modes_kept(jax.random.fold_in(streams_of[4], 71), part),
    }


precise = lax.Precision.HIGHEST

def hann_window(frames):
    steps = jnp.arange(frames, dtype=jnp.int32).astype(jnp.float32)
    shape = 0.5 - 0.5 * jnp.cos(2.0 * math.pi / frames * steps)
    return shape / jnp.sqrt(jnp.sum(shape * shape))

def unpack_pairs(z_re, z_im, offsets):
    frames = z_re.shape[0]
    half = frames // 2
    mirror_re = jnp.roll(jnp.flip(z_re, 0), 1, 0)[:half]
    mirror_im = jnp.roll(jnp.flip(z_im, 0), 1, 0)[:half]
    z_re = z_re[:half]
    z_im = z_im[:half]
    first_re = 0.5 * (z_re + mirror_re)
    first_im = 0.5 * (z_im - mirror_im)
    second_re = 0.5 * (z_im + mirror_im)
    second_im = 0.5 * (mirror_re - z_re)
    bins = jnp.arange(half, dtype=jnp.int32)
    phase = (bins[:, None] * offsets[None, :] % frames).astype(jnp.float32) * (2.0 * math.pi / frames)
    cos_part = jnp.cos(phase)[:, :, None]
    sin_part = jnp.sin(phase)[:, :, None]
    real_part = jnp.stack([first_re * cos_part + first_im * sin_part, second_re * cos_part + second_im * sin_part], axis=2)
    imag_part = jnp.stack([first_im * cos_part - first_re * sin_part, second_im * cos_part - second_re * sin_part], axis=2)
    return jnp.stack([real_part, imag_part], axis=2)

def gram_of(spectra, points):
    u_re = spectra[:, :, 0]
    u_im = spectra[:, :, 1]
    g_re = jnp.einsum('kbwp,kcwp->kbc', u_re, u_re, precision=precise) + jnp.einsum('kbwp,kcwp->kbc', u_im, u_im, precision=precise)
    g_im = jnp.einsum('kbwp,kcwp->kbc', u_re, u_im, precision=precise) - jnp.einsum('kbwp,kcwp->kbc', u_im, u_re, precision=precise)
    return jnp.stack([g_re, g_im], axis=1) / points

def complex_product(a_re, a_im, b_re, b_im):
    out_re = jnp.einsum('kij,kjm->kim', a_re, b_re, precision=precise) - jnp.einsum('kij,kjm->kim', a_im, b_im, precision=precise)
    out_im = jnp.einsum('kij,kjm->kim', a_re, b_im, precision=precise) + jnp.einsum('kij,kjm->kim', a_im, b_re, precision=precise)
    return (out_re, out_im)

def leading_basis(gram):
    g_re = gram[:, 0]
    g_im = gram[:, 1]
    number = g_re.shape[0]
    blocks = g_re.shape[1]
    q_re = jnp.broadcast_to(jnp.eye(blocks, M, dtype=jnp.float32), (number, blocks, M))
    q_im = jnp.zeros_like(q_re)
    for sweep_index in range(ITERS):
        y_re, y_im = complex_product(g_re, g_im, q_re, q_im)
        done_re = []
        done_im = []
        for column in range(M):
            v_re = y_re[:, :, column]
            v_im = y_im[:, :, column]
            for earlier in range(column):
                p_re = done_re[earlier]
                p_im = done_im[earlier]
                proj_re = lax.optimization_barrier(jnp.sum(p_re * v_re + p_im * v_im, axis=1, keepdims=True))
                proj_im = lax.optimization_barrier(jnp.sum(p_re * v_im - p_im * v_re, axis=1, keepdims=True))
                v_re = v_re - (proj_re * p_re - proj_im * p_im)
                v_im = v_im - (proj_re * p_im + proj_im * p_re)
            length = jnp.sqrt(lax.optimization_barrier(jnp.sum(v_re * v_re + v_im * v_im, axis=1, keepdims=True)))
            done_re.append(v_re / length)
            done_im.append(v_im / length)
        q_re = jnp.stack(done_re, axis=2)
        q_im = jnp.stack(done_im, axis=2)
    gq_re, gq_im = complex_product(g_re, g_im, q_re, q_im)
    energy = lax.optimization_barrier(jnp.sum(q_re * gq_re + q_im * gq_im, axis=1))
    return (jnp.stack([q_re, q_im], axis=1), energy)

def project(spectra, basis, energy, kept):
    u_re = spectra[:, :, 0]
    u_im = spectra[:, :, 1]
    q_re = basis[:, 0]
    q_im = basis[:, 1]
    m_re = jnp.einsum('kbwp,kbm->kmwp', u_re, q_re, precision=precise) - jnp.einsum('kbwp,kbm->kmwp', u_im, q_im, precision=precise)
    m_im = jnp.einsum('kbwp,kbm->kmwp', u_re, q_im, precision=precise) + jnp.einsum('kbwp,kbm->kmwp', u_im, q_re, precision=precise)
    live = (jnp.arange(M, dtype=jnp.int32)[None, :] < kept[:, None]).astype(jnp.float32)
    factor = (live / jnp.sqrt(energy))[:, :, None, None]
    return jnp.stack([m_re * factor, m_im * factor], axis=2)

def reference(signal, offsets, pairing, modes_kept):
    first_cols = pairing[0::2]
    second_cols = pairing[1::2]
    window = hann_window(NF)[:, None, None]
    block_pairs = math.gcd(NPAIR, 1024)
    block_total = NPAIR // block_pairs

    def spectra_of(block_index):
        cols_first = lax.dynamic_slice_in_dim(first_cols, block_index * block_pairs, block_pairs)
        cols_second = lax.dynamic_slice_in_dim(second_cols, block_index * block_pairs, block_pairs)
        part_re = jnp.take(signal, cols_first, axis=2) * window
        part_im = jnp.take(signal, cols_second, axis=2) * window
        spectrum = jnp.fft.fft(lax.complex(part_re, part_im), axis=0)
        return unpack_pairs(jnp.real(spectrum), jnp.imag(spectrum), offsets)

    def accumulate(carry, block_index):
        return (carry + gram_of(spectra_of(block_index), P_SIZE), None)
    start_gram = jnp.zeros((KB, 2, NB, NB), jnp.float32)
    gram, unused = lax.scan(accumulate, start_gram, jnp.arange(block_total, dtype=jnp.int32))
    basis, energy = leading_basis(gram)

    def modes_of(block_index):
        return project(spectra_of(block_index), basis, energy, modes_kept)
    pieces = lax.map(modes_of, jnp.arange(block_total, dtype=jnp.int32))
    modes = jnp.moveaxis(pieces, 0, 4).reshape(KB, M, 2, 2, NPAIR)
    return (energy, modes)
```

```python
import math

import jax
import jax.numpy as jnp
import numpy as np
from jax import lax
from jax.sharding import PartitionSpec as P

MODES = 4
ITERS = 3
precise = lax.Precision.HIGHEST


def transform_table(frames):
    steps = np.arange(frames)
    shape = 0.5 - 0.5 * np.cos(2.0 * np.pi * steps / frames)
    window = shape / np.sqrt(np.sum(shape * shape))
    phase = (steps[:, None] * np.arange(frames // 2)[None, :] % frames) * (2.0 * np.pi / frames)
    table = np.concatenate([np.cos(phase), -np.sin(phase)], axis=1) * window[:, None]
    return table.astype(np.float32)


def phase_table(offsets, bins, frames):
    steps = jnp.arange(bins, dtype=jnp.int32)[None, :] * offsets[:, None] % frames
    angle = steps.astype(jnp.float32) * (2.0 * math.pi / frames)
    return jnp.cos(angle), -jnp.sin(angle)


def sum_over(values, axis):
    size = lax.axis_size(axis)
    if size & (size - 1):
        return lax.psum(values, axis)
    step = 1
    while step < size:
        values = values + lax.ppermute(values, axis, [(i, i ^ step) for i in range(size)])
        step *= 2
    return values


def cmul(a, b):
    return a[0] * b[0] - a[1] * b[1], a[0] * b[1] + a[1] * b[0]


def cdot(a, b):
    return (
        jnp.sum(a[0] * b[0] + a[1] * b[1], axis=0, keepdims=True),
        jnp.sum(a[0] * b[1] - a[1] * b[0], axis=0, keepdims=True),
    )


def times_gram(g, v):
    re = jnp.sum(g[0] * v[0][None] - g[1] * v[1][None], axis=1)
    im = jnp.sum(g[0] * v[1][None] + g[1] * v[0][None], axis=1)
    return re, im


def leading_basis(g):
    blocks, bins = g[0].shape[0], g[0].shape[-1]
    ys = [(g[0][:, m], g[1][:, m]) for m in range(MODES)]
    for sweep in range(ITERS):
        done = []
        for v in ys:
            for q in done:
                part = cmul(cdot(q, v), q)
                v = (v[0] - part[0], v[1] - part[1])
            length = jnp.sqrt(jnp.sum(v[0] * v[0] + v[1] * v[1], axis=0, keepdims=True))
            done.append((v[0] / length, v[1] / length))
        ys = [times_gram(g, q) for q in done]
    energy = jnp.concatenate([cdot(q, y)[0] for q, y in zip(done, ys)], axis=0)
    return done, energy


def local(signal, offsets, pairing, modes_kept):
    rows, blocks, points = signal.shape
    ranks = lax.axis_size("freq")
    rank = lax.axis_index("freq")
    frames = rows * ranks
    bins = frames // 2
    own = points // ranks
    order = pairing.reshape(ranks, own // 2, 2).transpose(0, 2, 1).reshape(-1)
    packed = jnp.take(signal, order, axis=2).reshape(rows, blocks, ranks, own)
    packed = packed.transpose(2, 0, 1, 3)
    series = lax.all_to_all(packed, "freq", split_axis=0, concat_axis=0, tiled=True)
    series = series.reshape(frames, blocks * own)
    table = jnp.asarray(transform_table(frames))
    spectra = lax.dot_general(series, table, (((0,), (0,)), ((), ())), precision=precise)
    spectra = spectra.reshape(blocks, own, 2, bins)
    u = (spectra[:, :, 0], spectra[:, :, 1])
    pairs = []
    for b in range(blocks):
        for e in range(b, blocks):
            pairs.append(jnp.sum(u[0][b] * u[0][e] + u[1][b] * u[1][e], axis=0))
            if e > b:
                pairs.append(jnp.sum(u[0][b] * u[1][e] - u[1][b] * u[0][e], axis=0))
    sums = sum_over(jnp.stack(pairs, axis=0), "freq") * (1.0 / points)
    g_re = [[None] * blocks for _ in range(blocks)]
    g_im = [[None] * blocks for _ in range(blocks)]
    at = 0
    for b in range(blocks):
        for e in range(b, blocks):
            g_re[b][e] = g_re[e][b] = sums[at]
            at += 1
            if e > b:
                g_im[b][e], g_im[e][b] = sums[at], -sums[at]
                at += 1
            else:
                g_im[b][b] = jnp.zeros_like(sums[0])
    g = (
        jnp.stack([jnp.stack(row) for row in g_re]),
        jnp.stack([jnp.stack(row) for row in g_im]),
    )
    turn = phase_table(offsets, bins, frames)
    both = cmul((turn[0][:, None], -turn[1][:, None]), (turn[0][None], turn[1][None]))
    basis, energy = leading_basis(cmul(both, g))
    live = jnp.arange(MODES, dtype=jnp.int32)[:, None] < modes_kept[None, :]
    factor = live.astype(jnp.float32) / jnp.sqrt(energy)
    modes = []
    for m in range(MODES):
        q = cmul(turn, basis[m])
        q = (q[0] * factor[m], q[1] * factor[m])
        re = jnp.sum(u[0] * q[0][:, None] - u[1] * q[1][:, None], axis=0)
        im = jnp.sum(u[0] * q[1][:, None] + u[1] * q[0][:, None], axis=0)
        modes.append(jnp.stack([re, im]))
    modes = jnp.stack(modes).reshape(MODES, 2, 2, own // 2, bins)
    held = lax.dynamic_slice_in_dim(energy, rank * (bins // ranks), bins // ranks, axis=1)
    return held.T, modes.transpose(4, 0, 1, 2, 3)


def solution(mesh):
    placed = (P("freq", None, "groups"), P(), P("groups"), P())
    return jax.shard_map(
        local,
        mesh=mesh,
        in_specs=placed,
        out_specs=(P("freq", "groups"), P(None, None, None, None, ("groups", "freq"))),
        check_vma=False,
    )
```

```python
import math

import jax
import jax.numpy as jnp
import ml_dtypes
import numpy as np
from jax import lax
from jax.experimental import pallas as pl
from jax.experimental.pallas import tpu as pltpu
from jax.sharding import PartitionSpec as P

MODES = 4
ITERS = 3
precise = lax.Precision.HIGHEST


def transform_table(frames):
    steps = np.arange(frames)
    shape = 0.5 - 0.5 * np.cos(2.0 * np.pi * steps / frames)
    window = shape / np.sqrt(np.sum(shape * shape))
    phase = (steps[:, None] * np.arange(frames // 2)[None, :] % frames) * (2.0 * np.pi / frames)
    table = np.concatenate([np.cos(phase), -np.sin(phase)], axis=1) * window[:, None]
    return table.astype(np.float32)


def phase_table(offsets, bins, frames):
    steps = jnp.arange(bins, dtype=jnp.int32)[None, :] * offsets[:, None] % frames
    angle = steps.astype(jnp.float32) * (2.0 * math.pi / frames)
    return jnp.cos(angle), -jnp.sin(angle)


def sum_over(values, axis):
    size = lax.axis_size(axis)
    if size & (size - 1):
        return lax.psum(values, axis)
    step = 1
    while step < size:
        values = values + lax.ppermute(values, axis, [(i, i ^ step) for i in range(size)])
        step *= 2
    return values


def cmul(a, b):
    return a[0] * b[0] - a[1] * b[1], a[0] * b[1] + a[1] * b[0]


def cdot(a, b):
    return (
        jnp.sum(a[0] * b[0] + a[1] * b[1], axis=0, keepdims=True),
        jnp.sum(a[0] * b[1] - a[1] * b[0], axis=0, keepdims=True),
    )


def times_gram(g, v):
    re = jnp.sum(g[0] * v[0][None] - g[1] * v[1][None], axis=1)
    im = jnp.sum(g[0] * v[1][None] + g[1] * v[0][None], axis=1)
    return re, im


def leading_basis(g):
    blocks, bins = g[0].shape[0], g[0].shape[-1]
    ys = [(g[0][:, m], g[1][:, m]) for m in range(MODES)]
    for sweep in range(ITERS):
        done = []
        for v in ys:
            for q in done:
                part = cmul(cdot(q, v), q)
                v = (v[0] - part[0], v[1] - part[1])
            length = jnp.sqrt(jnp.sum(v[0] * v[0] + v[1] * v[1], axis=0, keepdims=True))
            done.append((v[0] / length, v[1] / length))
        ys = [times_gram(g, q) for q in done]
    energy = jnp.concatenate([cdot(q, y)[0] for q, y in zip(done, ys)], axis=0)
    return done, energy


LANES = 128
GROUP = 4
VMEM = pltpu.CompilerParams(vmem_limit_bytes=48 * 2**20)


def split_table(frames):
    table = transform_table(frames).reshape(frames, 2, -1, LANES)
    table = table.transpose(0, 2, 1, 3).reshape(frames, frames)
    high = table.astype(ml_dtypes.bfloat16)
    low = (table - high.astype(np.float32)).astype(ml_dtypes.bfloat16)
    return high, low


def two_terms(x):
    high = x.astype(jnp.bfloat16)
    return high, (x - high.astype(jnp.float32)).astype(jnp.bfloat16)


def three_terms(x):
    high, rest = x.astype(jnp.bfloat16), None
    rest = x - high.astype(jnp.float32)
    mid = rest.astype(jnp.bfloat16)
    return high, mid, (rest - mid.astype(jnp.float32)).astype(jnp.bfloat16)


def dot(a, b):
    return jnp.dot(a, b, preferred_element_type=jnp.float32)


def pack_kernel(blocks, strips, dst, *rest):
    signals, pairing, rest = rest[:strips], rest[strips], rest[strips + 1 :]
    outs, one_row = rest[:GROUP], rest[GROUP]
    step = pl.program_id(0)
    rows = signals[0].shape[0] // blocks
    depth = strips * LANES

    @pl.when(step == 0)
    def _():
        place = lax.broadcasted_iota(jnp.int32, (LANES, LANES), 1)
        source = lax.broadcasted_iota(jnp.int32, (LANES, LANES), 0)
        half = LANES // 2
        wanted = jnp.where(place < half, 2 * place, 2 * (place - half) + 1)
        turn = (wanted == source).astype(jnp.float32).astype(jnp.bfloat16)
        lines = pairing[...]
        upper = (lines >> 5).astype(jnp.float32).astype(jnp.bfloat16)
        lower = (lines & 31).astype(jnp.float32).astype(jnp.bfloat16)
        one_row[...] = (dot(upper, turn) * 32.0 + dot(lower, turn)).astype(jnp.int32)

    x = jnp.concatenate(
        [
            jnp.concatenate([strip[pl.ds(b, rows, stride=blocks), :] for strip in signals], axis=1)
            for b in range(blocks)
        ],
        axis=0,
    )
    terms = three_terms(x)
    source = lax.broadcasted_iota(jnp.int32, (depth, LANES), 0) + step * depth
    for at in range(GROUP):
        line = one_row[pl.ds(dst[at], 1), :]
        pick = jnp.where(source == line, 1.0, 0.0).astype(jnp.bfloat16)
        got = dot(terms[0], pick) + dot(terms[1], pick) + dot(terms[2], pick)
        for b in range(blocks):
            part = got[b * rows : (b + 1) * rows]
            spot = (slice(None), slice(b * LANES, (b + 1) * LANES))

            @pl.when(step == 0)
            def _():
                outs[at][spot] = part

            @pl.when(step > 0)
            def _():
                outs[at][spot] += part


def pack(signal, pairing, dst):
    rows, blocks, points = signal.shape
    strips = 4
    depth = strips * LANES
    width = blocks * LANES
    return pl.pallas_call(
        lambda *refs: pack_kernel(blocks, strips, *refs),
        grid_spec=pltpu.PrefetchScalarGridSpec(
            num_scalar_prefetch=1,
            grid=(points // depth,),
            in_specs=[
                pl.BlockSpec((rows * blocks, LANES), lambda i, d, n=n: (0, strips * i + n))
                for n in range(strips)
            ]
            + [pl.BlockSpec((points // LANES, LANES), lambda i, d: (0, 0))],
            out_specs=[pl.BlockSpec((rows, width), lambda i, d: (0, 0))] * GROUP,
            scratch_shapes=[pltpu.VMEM((points // LANES, LANES), jnp.int32)],
        ),
        out_shape=[jax.ShapeDtypeStruct((rows, width), jnp.float32)] * GROUP,
        compiler_params=VMEM,
        cost_estimate=pl.CostEstimate(
            flops=6 * rows * blocks * points * GROUP * LANES, bytes_accessed=8 * 2**20, transcendentals=0
        ),
    )(dst, *[signal.reshape(rows * blocks, points)] * strips, pairing.reshape(-1, LANES))


def pair_list(blocks):
    return [(b, e) for b in range(blocks) for e in range(b, blocks)]


def gram_tile(re, im, blocks, gram):
    own = re.shape[0] // blocks
    at = 0
    todo = []
    for b, e in pair_list(blocks):
        todo.append((at, b, e))
        at += 1 if b == e else 2
    for first in range(0, len(todo), 18):
        chunk = todo[first : first + 18]
        used = sorted({b for _, b, _ in chunk} | {e for _, _, e in chunk})

        def body(i, sums):
            start = pl.multiple_of(i * 8, 8)
            u = {b: (re[pl.ds(b * own + start, 8), :], im[pl.ds(b * own + start, 8), :]) for b in used}
            out = []
            for _, b, e in chunk:
                (br, bi), (er, ei) = u[b], u[e]
                out.append(br * er + bi * ei)
                if b != e:
                    out.append(br * ei - bi * er)
            return tuple(s + o for s, o in zip(sums, out))

        count = sum(1 if b == e else 2 for _, b, e in chunk)
        zero = jnp.zeros((8, re.shape[1]), jnp.float32)
        sums = lax.fori_loop(0, own // 8, body, (zero,) * count)
        base = chunk[0][0]
        for n, value in enumerate(sums):
            gram[base + n : base + n + 1, :] = jnp.sum(value, axis=0, keepdims=True)


def spectra_kernel(blocks, count, more, with_gram, src, *refs):
    xs, (high, low), refs = refs[:count], refs[count : count + 2], refs[count + 2 :]
    prev, refs = (refs[:2], refs[2:]) if more else (None, refs)
    (re, im), refs = refs[:2], refs[2:]
    gram, refs = (refs[0], refs[1:]) if with_gram else (None, refs)
    x_high, x_low = refs
    rows = xs[0].shape[0]

    @pl.when(pl.program_id(0) == 0)
    def _():
        for g in range(0, count, GROUP):
            x = jnp.concatenate([x[...] for x in xs[g : g + GROUP]], axis=0)
            spot = (slice(None), slice(g * rows, (g + GROUP) * rows))
            x_high[spot], x_low[spot] = two_terms(x.T)

    def table(ref):
        return jnp.concatenate(
            [ref[pl.ds(pl.multiple_of(src[n] * rows, rows), rows), :] for n in range(count)], axis=0
        )

    w_high, w_low = table(high), table(low)
    got = dot(x_high[...], w_high) + dot(x_low[...], w_high) + dot(x_high[...], w_low)
    if more:
        re[...] = prev[0][...] + got[:, :LANES]
        im[...] = prev[1][...] + got[:, LANES:]
    else:
        re[...] = got[:, :LANES]
        im[...] = got[:, LANES:]
    if with_gram:
        gram_tile(re, im, blocks, gram)


def spectra(blocks, xs, src, tables, prev=None, with_gram=False):
    rows, width = xs[0].shape
    frames = tables[0].shape[0]
    bins = frames // 2
    count = len(xs)
    held = pl.BlockSpec((width, LANES), lambda i, s: (0, i))
    shape = jax.ShapeDtypeStruct((width, bins), jnp.float32)
    in_specs = [pl.BlockSpec((rows, width), lambda i, s: (0, 0))] * count
    in_specs += [pl.BlockSpec((frames, 2 * LANES), lambda i, s: (0, i))] * 2
    out_specs, out_shape = [held] * 2, [shape] * 2
    if prev is not None:
        in_specs += [held] * 2
    if with_gram:
        out_specs.append(pl.BlockSpec((blocks * blocks, LANES), lambda i, s: (0, i)))
        out_shape.append(jax.ShapeDtypeStruct((blocks * blocks, bins), jnp.float32))
    return pl.pallas_call(
        lambda *refs: spectra_kernel(blocks, count, prev is not None, with_gram, *refs),
        grid_spec=pltpu.PrefetchScalarGridSpec(
            num_scalar_prefetch=1,
            grid=(bins // LANES,),
            in_specs=in_specs,
            out_specs=out_specs,
            scratch_shapes=[pltpu.VMEM((width, count * rows), jnp.bfloat16)] * 2,
        ),
        out_shape=out_shape,
        compiler_params=VMEM,
        cost_estimate=pl.CostEstimate(
            flops=6 * width * frames * count * rows, bytes_accessed=12 * 2**20, transcendentals=0
        ),
    )(src, *xs, *tables, *(prev or ()))


def gram_of(u, blocks):
    pairs = []
    for b, e in pair_list(blocks):
        pairs.append(jnp.sum(u[0][b] * u[0][e] + u[1][b] * u[1][e], axis=0))
        if e > b:
            pairs.append(jnp.sum(u[0][b] * u[1][e] - u[1][b] * u[0][e], axis=0))
    return jnp.stack(pairs, axis=0)


def plain_spectra(signal, pairing):
    rows, blocks, points = signal.shape
    ranks = lax.axis_size("freq")
    frames, own = rows * ranks, points // ranks
    order = pairing.reshape(ranks, own // 2, 2).transpose(0, 2, 1).reshape(-1)
    packed = jnp.take(signal, order, axis=2).reshape(rows, blocks, ranks, own)
    packed = packed.transpose(2, 0, 1, 3)
    series = lax.all_to_all(packed, "freq", split_axis=0, concat_axis=0, tiled=True)
    series = series.reshape(frames, blocks * own)
    table = jnp.asarray(transform_table(frames))
    both = lax.dot_general(series, table, (((0,), (0,)), ((), ())), precision=precise)
    both = both.reshape(blocks, own, 2, frames // 2)
    u = (both[:, :, 0], both[:, :, 1])
    return u, gram_of(u, blocks)


def tiled_spectra(signal, pairing):
    rows, blocks, points = signal.shape
    ranks = lax.axis_size("freq")
    rank = lax.axis_index("freq")
    tables = [jnp.asarray(t) for t in split_table(rows * ranks)]
    near = jnp.arange(GROUP, dtype=jnp.int32)
    groups = ranks // GROUP
    order = sorted(range(groups), key=lambda s: (-(s & -2), s & 1)) if groups > 2 else [1, 0]
    order = order[:-2] + [1, 0] if groups > 2 else order
    got, last = {}, None
    for s in order:
        if last is not None:
            signal, last = lax.optimization_barrier((signal, last))
        parts = last = pack(signal, pairing, rank ^ (s * GROUP + near))
        got[s] = [
            part if s * GROUP + n == 0 else lax.ppermute(part, "freq", [(i, i ^ (s * GROUP + n)) for i in range(ranks)])
            for n, part in enumerate(parts)
        ]
    own = [0, 1]
    far = [s for s in order if s not in own]
    total = spectra(blocks, got[0] + got[1], rank ^ jnp.arange(2 * GROUP, dtype=jnp.int32), tables)
    for s in far:
        total = spectra(
            blocks, got[s], rank ^ (s * GROUP + near), tables, total[:2], with_gram=s == far[-1]
        )
    re, im, gram = total
    shape = (blocks, LANES, -1)
    return (re.reshape(shape), im.reshape(shape)), gram


def local(signal, offsets, pairing, modes_kept):
    rows, blocks, points = signal.shape
    ranks = lax.axis_size("freq")
    rank = lax.axis_index("freq")
    frames = rows * ranks
    bins = frames // 2
    own = points // ranks
    tiled = own == LANES and rows % 64 == 0 and ranks == 4 * GROUP and points % 512 == 0
    u, gram = (tiled_spectra if tiled else plain_spectra)(signal, pairing)
    sums = sum_over(gram, "freq") * (1.0 / points)
    g_re = [[None] * blocks for _ in range(blocks)]
    g_im = [[None] * blocks for _ in range(blocks)]
    at = 0
    for b in range(blocks):
        for e in range(b, blocks):
            g_re[b][e] = g_re[e][b] = sums[at]
            at += 1
            if e > b:
                g_im[b][e], g_im[e][b] = sums[at], -sums[at]
                at += 1
            else:
                g_im[b][b] = jnp.zeros_like(sums[0])
    g = (
        jnp.stack([jnp.stack(row) for row in g_re]),
        jnp.stack([jnp.stack(row) for row in g_im]),
    )
    turn = phase_table(offsets, bins, frames)
    both = cmul((turn[0][:, None], -turn[1][:, None]), (turn[0][None], turn[1][None]))
    basis, energy = leading_basis(cmul(both, g))
    live = jnp.arange(MODES, dtype=jnp.int32)[:, None] < modes_kept[None, :]
    factor = live.astype(jnp.float32) / jnp.sqrt(energy)
    modes = []
    for m in range(MODES):
        q = cmul(turn, basis[m])
        q = (q[0] * factor[m], q[1] * factor[m])
        re = jnp.sum(u[0] * q[0][:, None] - u[1] * q[1][:, None], axis=0)
        im = jnp.sum(u[0] * q[1][:, None] + u[1] * q[0][:, None], axis=0)
        modes.append(jnp.stack([re, im]))
    modes = jnp.stack(modes).reshape(MODES, 2, 2, own // 2, bins)
    held = lax.dynamic_slice_in_dim(energy, rank * (bins // ranks), bins // ranks, axis=1)
    return held.T, modes.transpose(4, 0, 1, 2, 3)


def solution(mesh):
    placed = (P("freq", None, "groups"), P(), P("groups"), P())
    return jax.shard_map(
        local,
        mesh=mesh,
        in_specs=placed,
        out_specs=(P("freq", "groups"), P(None, None, None, None, ("groups", "freq"))),
        check_vma=False,
    )
```

```python
import math

import jax
import jax.numpy as jnp
import ml_dtypes
import numpy as np
from jax import lax
from jax.experimental import pallas as pl
from jax.experimental.pallas import tpu as pltpu
from jax.sharding import PartitionSpec as P

MODES = 4
ITERS = 3
precise = lax.Precision.HIGHEST


def transform_table(frames):
    steps = np.arange(frames)
    shape = 0.5 - 0.5 * np.cos(2.0 * np.pi * steps / frames)
    window = shape / np.sqrt(np.sum(shape * shape))
    phase = (steps[:, None] * np.arange(frames // 2)[None, :] % frames) * (2.0 * np.pi / frames)
    table = np.concatenate([np.cos(phase), -np.sin(phase)], axis=1) * window[:, None]
    return table.astype(np.float32)


def phase_table(offsets, bins, frames):
    steps = jnp.arange(bins, dtype=jnp.int32)[None, :] * offsets[:, None] % frames
    angle = steps.astype(jnp.float32) * (2.0 * math.pi / frames)
    return jnp.cos(angle), -jnp.sin(angle)


def sum_over(values, axis):
    size = lax.axis_size(axis)
    if size & (size - 1):
        return lax.psum(values, axis)
    step = 1
    while step < size:
        values = values + lax.ppermute(values, axis, [(i, i ^ step) for i in range(size)])
        step *= 2
    return values


def cmul(a, b):
    return a[0] * b[0] - a[1] * b[1], a[0] * b[1] + a[1] * b[0]


def cdot(a, b):
    return (
        jnp.sum(a[0] * b[0] + a[1] * b[1], axis=0, keepdims=True),
        jnp.sum(a[0] * b[1] - a[1] * b[0], axis=0, keepdims=True),
    )


def times_gram(g, v):
    re = jnp.sum(g[0] * v[0][None] - g[1] * v[1][None], axis=1)
    im = jnp.sum(g[0] * v[1][None] + g[1] * v[0][None], axis=1)
    return re, im


def leading_basis(g):
    blocks, bins = g[0].shape[0], g[0].shape[-1]
    ys = [(g[0][:, m], g[1][:, m]) for m in range(MODES)]
    for sweep in range(ITERS):
        done = []
        for v in ys:
            for q in done:
                part = cmul(cdot(q, v), q)
                v = (v[0] - part[0], v[1] - part[1])
            length = jnp.sqrt(jnp.sum(v[0] * v[0] + v[1] * v[1], axis=0, keepdims=True))
            done.append((v[0] / length, v[1] / length))
        ys = [times_gram(g, q) for q in done]
    energy = jnp.concatenate([cdot(q, y)[0] for q, y in zip(done, ys)], axis=0)
    return done, energy


LANES = 128
GROUP = 4
VMEM = pltpu.CompilerParams(vmem_limit_bytes=60 * 2**20)
SMALL = pltpu.CompilerParams(vmem_limit_bytes=32 * 2**20)


def split_table(frames):
    table = transform_table(frames).reshape(frames, 2, -1, LANES)
    table = table.transpose(0, 2, 1, 3).reshape(frames, frames)
    high = table.astype(ml_dtypes.bfloat16)
    low = (table - high.astype(np.float32)).astype(ml_dtypes.bfloat16)
    return high, low


def two_terms(x):
    high = x.astype(jnp.bfloat16)
    return high, (x - high.astype(jnp.float32)).astype(jnp.bfloat16)


def three_terms(x):
    high, rest = x.astype(jnp.bfloat16), None
    rest = x - high.astype(jnp.float32)
    mid = rest.astype(jnp.bfloat16)
    return high, mid, (rest - mid.astype(jnp.float32)).astype(jnp.bfloat16)


def dot(a, b):
    return jnp.dot(a, b, preferred_element_type=jnp.float32)


def pack_kernel(blocks, first, count, strips, *refs):
    signals, pairing, out, one_row, total = refs[:strips], *refs[strips:]
    step = pl.program_id(0)
    rows = signals[0].shape[0] // blocks
    ranks = out.shape[0]
    depth = strips * LANES

    @pl.when(step == 0)
    def _():
        place = lax.broadcasted_iota(jnp.int32, (LANES, LANES), 1)
        source = lax.broadcasted_iota(jnp.int32, (LANES, LANES), 0)
        half = LANES // 2
        wanted = jnp.where(place < half, 2 * place, 2 * (place - half) + 1)
        turn = (wanted == source).astype(jnp.float32).astype(jnp.bfloat16)
        lines = pairing[...]
        upper = (lines >> 5).astype(jnp.float32).astype(jnp.bfloat16)
        lower = (lines & 31).astype(jnp.float32).astype(jnp.bfloat16)
        one_row[...] = (dot(upper, turn) * 32.0 + dot(lower, turn)).astype(jnp.int32)
        total[...] = jnp.zeros_like(total)

    x = jnp.concatenate(
        [
            jnp.concatenate([strip[pl.ds(b, rows, stride=blocks), :] for strip in signals], axis=1)
            for b in range(first, first + count)
        ],
        axis=0,
    )
    terms = three_terms(x)
    source = lax.broadcasted_iota(jnp.int32, (depth, LANES), 0) + step * depth
    for at in range(0, ranks, GROUP):
        pick = jnp.concatenate(
            [
                jnp.where(source == one_row[n : n + 1, :], 1.0, 0.0).astype(jnp.bfloat16)
                for n in range(at, at + GROUP)
            ],
            axis=1,
        )
        spot = (slice(None), slice(at * LANES, (at + GROUP) * LANES))
        total[spot] += dot(terms[0], pick) + dot(terms[1], pick) + dot(terms[2], pick)

    @pl.when(step == pl.num_programs(0) - 1)
    def _():
        for n in range(ranks):
            for b in range(count):
                out[n, :, b * LANES : (b + 1) * LANES] = total[
                    b * rows : (b + 1) * rows, n * LANES : (n + 1) * LANES
                ]


def pack(signal, pairing, first, count):
    rows, blocks, points = signal.shape
    strips = 4
    ranks = points // LANES
    shape = (ranks, rows, count * LANES)
    return pl.pallas_call(
        lambda *refs: pack_kernel(blocks, first, count, strips, *refs),
        grid=(points // (strips * LANES),),
        in_specs=[
            pl.BlockSpec((rows * blocks, LANES), lambda i, n=n: (0, strips * i + n))
            for n in range(strips)
        ]
        + [pl.BlockSpec((ranks, LANES), lambda i: (0, 0))],
        out_specs=pl.BlockSpec(shape, lambda i: (0, 0, 0)),
        scratch_shapes=[
            pltpu.VMEM((ranks, LANES), jnp.int32),
            pltpu.VMEM((rows * count, points), jnp.float32),
        ],
        out_shape=jax.ShapeDtypeStruct(shape, jnp.float32),
        compiler_params=VMEM,
        cost_estimate=pl.CostEstimate(
            flops=6 * rows * count * points * points, bytes_accessed=8 * 2**20, transcendentals=0
        ),
    )(*[signal.reshape(rows * blocks, points)] * strips, pairing.reshape(-1, LANES))


def pair_list(blocks):
    return [(b, e) for b in range(blocks) for e in range(b, blocks)]


def gram_tile(parts, blocks, gram):
    where = []
    for re, im in parts:
        where += [(re, im, n * LANES) for n in range(re.shape[0] // LANES)]
    fresh = len(where)
    start = fresh - parts[-1][0].shape[0] // LANES
    todo = [(b, e) for e in range(start, fresh) for b in range(e + 1)]
    most = 14
    for first in range(0, len(todo), most):
        chunk = todo[first : first + most]
        used = sorted({b for b, _ in chunk} | {e for _, e in chunk})

        def body(i, sums):
            spot = pl.multiple_of(i * 8, 8)
            u = {}
            for b in used:
                re, im, base = where[b]
                u[b] = (re[pl.ds(base + spot, 8), :], im[pl.ds(base + spot, 8), :])
            out = []
            for b, e in chunk:
                (br, bi), (er, ei) = u[b], u[e]
                out.append(br * er + bi * ei)
                if b != e:
                    out.append(br * ei - bi * er)
            return tuple(s + o for s, o in zip(sums, out))

        rows = []
        for b, e in chunk:
            rows += [e * blocks + b] if b == e else [e * blocks + b, b * blocks + e]
        zero = jnp.zeros((8, gram.shape[1]), jnp.float32)
        sums = lax.fori_loop(0, LANES // 8, body, (zero,) * len(rows))
        for row, value in zip(rows, sums):
            gram[row : row + 1, :] = jnp.sum(value, axis=0, keepdims=True)


def spectra_kernel(blocks, others, final, core, x, high, low, *refs):
    parts = [(refs[2 * n], refs[2 * n + 1]) for n in range(others)]
    refs = refs[2 * others :]
    before, refs = (refs[0], refs[1:]) if others else (None, refs)
    (re, im), grams, (x_high, x_low, gram) = refs[:2], refs[2:-3], refs[-3:]
    step = pl.program_id(0)

    @pl.when(step == 0)
    def _():
        x_high[...], x_low[...] = two_terms(x[...].T)

    got = dot(x_high[...], high[...]) + dot(x_low[...], high[...]) + dot(x_high[...], low[...])
    re[...] = got[:, :LANES]
    im[...] = got[:, LANES:]
    gram[...] = before[...] if others else jnp.zeros_like(gram)
    gram_tile(parts + [(re, im)], blocks, gram)
    if final:
        half = step // (pl.num_programs(0) // 2)
        lane = pl.multiple_of(step % (pl.num_programs(0) // 2) * LANES, LANES)

        @pl.when(half == core[0])
        def _():
            grams[0][:, pl.ds(lane, LANES)] = gram[...]

        @pl.when(half != core[0])
        def _():
            grams[1][:, pl.ds(lane, LANES)] = gram[...]
    else:
        grams[0][...] = gram[...]


def spectra(blocks, x, tables, core, others=(), before=None, final=False):
    frames, width = x.shape
    bins = frames // 2
    held = pl.BlockSpec((width, LANES), lambda i, c: (0, i))
    shape = jax.ShapeDtypeStruct((width, bins), jnp.float32)
    flat = [a for part in others for a in part] + ([before] if others else [])
    in_specs = [pl.BlockSpec((frames, width), lambda i, c: (0, 0))]
    in_specs += [pl.BlockSpec((frames, 2 * LANES), lambda i, c: (0, i))] * 2
    in_specs += [pl.BlockSpec((a.shape[0], LANES), lambda i, c: (0, i)) for a in flat]
    square = blocks * blocks
    if final:
        out_specs = [held] * 2 + [pl.BlockSpec((square, bins // 2), lambda i, c: (0, 0))] * 2
        out_shape = [shape] * 2 + [jax.ShapeDtypeStruct((square, bins // 2), jnp.float32)] * 2
    else:
        out_specs = [held] * 2 + [pl.BlockSpec((square, LANES), lambda i, c: (0, i))]
        out_shape = [shape] * 2 + [jax.ShapeDtypeStruct((square, bins), jnp.float32)]
    return pl.pallas_call(
        lambda *refs: spectra_kernel(blocks, len(others), final, *refs),
        grid_spec=pltpu.PrefetchScalarGridSpec(
            num_scalar_prefetch=1,
            grid=(bins // LANES,),
            in_specs=in_specs,
            out_specs=out_specs,
            scratch_shapes=[pltpu.VMEM((width, frames), jnp.bfloat16)] * 2
            + [pltpu.VMEM((square, LANES), jnp.float32)],
        ),
        out_shape=out_shape,
        compiler_params=SMALL,
        cost_estimate=pl.CostEstimate(
            flops=6 * width * frames * frames, bytes_accessed=12 * 2**20, transcendentals=0
        ),
    )(core, x, *tables, *flat)


def row_dot(a, b):
    return (
        jnp.sum(a[0] * b[0] + a[1] * b[1], axis=0, keepdims=True),
        jnp.sum(a[0] * b[1] - a[1] * b[0], axis=0, keepdims=True),
    )


def finish_kernel(blocks, points, parts, core, mine, other, turn_re, turn_im, kept, *refs):
    spectra_refs = [(refs[2 * n], refs[2 * n + 1]) for n in range(parts)]
    energy, modes, tiles, basis = refs[2 * parts :]
    step = pl.program_id(0)

    @pl.when(step == 0)
    def _():
        swap = core[0] == 1
        half = mine.shape[1]
        count = 2 * half // LANES
        for t in range(count):
            lane = slice(t * LANES % half, t * LANES % half + LANES)
            ours = jnp.logical_xor(swap, t * LANES >= half)
            tiles[t] = jnp.where(ours, other[:, lane], mine[:, lane]) * (1.0 / points)
        ph = (turn_re[...], turn_im[...])
        back = (ph[0], -ph[1])
        row = lax.broadcasted_iota(jnp.int32, ph[0].shape, 0)
        g = []
        for e in range(blocks):
            down = [tiles[t, e * blocks : (e + 1) * blocks, :] for t in range(count)]
            across = [tiles[t, pl.ds(e, blocks, stride=blocks), :] for t in range(count)]
            down, across = jnp.concatenate(down, axis=1), jnp.concatenate(across, axis=1)
            re = jnp.where(row <= e, down, across)
            im = jnp.where(row < e, across, jnp.where(row > e, -down, 0.0))
            column = (ph[0][e : e + 1], ph[1][e : e + 1])
            g.append(cmul(cmul(back, (re, im)), column))
        ys = g[:MODES]
        for sweep in range(ITERS):
            done = []
            for v in ys:
                for q in done:
                    part = cmul(row_dot(q, v), q)
                    v = (v[0] - part[0], v[1] - part[1])
                length = jnp.sqrt(jnp.sum(v[0] * v[0] + v[1] * v[1], axis=0, keepdims=True))
                done.append((v[0] / length, v[1] / length))
            ys = []
            for q in done:
                re, im = jnp.zeros_like(q[0]), jnp.zeros_like(q[0])
                for e in range(blocks):
                    part = cmul(g[e], (q[0][e : e + 1], q[1][e : e + 1]))
                    re, im = re + part[0], im + part[1]
                ys.append((re, im))
        for m, (q, y) in enumerate(zip(done, ys)):
            level = row_dot(q, y)[0]
            energy[m : m + 1, :] = level
            factor = jnp.where(kept[...] > m, 1.0, 0.0) / jnp.sqrt(level)
            re, im = cmul(ph, q)
            re, im = re * factor, im * factor
            for t in range(count):
                lane = slice(t * LANES, (t + 1) * LANES)
                basis[t, 2 * m * blocks : (2 * m + 1) * blocks, :] = re[:, lane]
                basis[t, (2 * m + 1) * blocks : (2 * m + 2) * blocks, :] = im[:, lane]

    where = []
    for re, im in spectra_refs:
        where += [(re, im, n * LANES) for n in range(re.shape[0] // LANES)]
    for m in range(MODES):
        total_re, total_im = None, None
        for b, (re, im, base) in enumerate(where):
            u = (re[base : base + LANES, :], im[base : base + LANES, :])
            q = [basis[step, pl.ds((2 * m + n) * blocks + b, 1), :] for n in (0, 1)]
            part = cmul(u, q)
            total_re = part[0] if b == 0 else total_re + part[0]
            total_im = part[1] if b == 0 else total_im + part[1]
        modes[m, 0] = total_re
        modes[m, 1] = total_im


def finish(blocks, points, core, mine, other, turn, kept, parts):
    square, half = mine.shape
    bins = 2 * half
    flat = [a for part in parts for a in part]
    whole = lambda a: pl.BlockSpec(a.shape, lambda i, c: (0, 0))
    kept = kept.reshape(1, bins)
    small = [mine, other, *turn, kept]
    return pl.pallas_call(
        lambda *refs: finish_kernel(blocks, points, len(parts), *refs),
        grid_spec=pltpu.PrefetchScalarGridSpec(
            num_scalar_prefetch=1,
            grid=(bins // LANES,),
            in_specs=[whole(a) for a in small]
            + [pl.BlockSpec((a.shape[0], LANES), lambda i, c: (0, i)) for a in flat],
            out_specs=[
                pl.BlockSpec((MODES, bins), lambda i, c: (0, 0)),
                pl.BlockSpec((MODES, 2, LANES, LANES), lambda i, c: (0, 0, 0, i)),
            ],
            scratch_shapes=[
                pltpu.VMEM((bins // LANES, square, LANES), jnp.float32),
                pltpu.VMEM((bins // LANES, 2 * MODES * blocks, LANES), jnp.float32),
            ],
        ),
        out_shape=[
            jax.ShapeDtypeStruct((MODES, bins), jnp.float32),
            jax.ShapeDtypeStruct((MODES, 2, LANES, bins), jnp.float32),
        ],
        compiler_params=SMALL,
        cost_estimate=pl.CostEstimate(
            flops=16 * MODES * blocks * LANES * bins, bytes_accessed=6 * 2**20, transcendentals=0
        ),
    )(core, *small, *flat)


def gram_of(u, blocks):
    pairs = []
    for b, e in pair_list(blocks):
        pairs.append(jnp.sum(u[0][b] * u[0][e] + u[1][b] * u[1][e], axis=0))
        if e > b:
            pairs.append(jnp.sum(u[0][b] * u[1][e] - u[1][b] * u[0][e], axis=0))
    return jnp.stack(pairs, axis=0)


def plain(signal, offsets, pairing, modes_kept):
    rows, blocks, points = signal.shape
    ranks = lax.axis_size("freq")
    rank = lax.axis_index("freq")
    frames = rows * ranks
    bins = frames // 2
    own = points // ranks
    order = pairing.reshape(ranks, own // 2, 2).transpose(0, 2, 1).reshape(-1)
    packed = jnp.take(signal, order, axis=2).reshape(rows, blocks, ranks, own)
    packed = packed.transpose(2, 0, 1, 3)
    series = lax.all_to_all(packed, "freq", split_axis=0, concat_axis=0, tiled=True)
    series = series.reshape(frames, blocks * own)
    table = jnp.asarray(transform_table(frames))
    spectra = lax.dot_general(series, table, (((0,), (0,)), ((), ())), precision=precise)
    spectra = spectra.reshape(blocks, own, 2, bins)
    u = (spectra[:, :, 0], spectra[:, :, 1])
    sums = sum_over(gram_of(u, blocks), "freq") * (1.0 / points)
    g_re = [[None] * blocks for _ in range(blocks)]
    g_im = [[None] * blocks for _ in range(blocks)]
    at = 0
    for b in range(blocks):
        for e in range(b, blocks):
            g_re[b][e] = g_re[e][b] = sums[at]
            at += 1
            if e > b:
                g_im[b][e], g_im[e][b] = sums[at], -sums[at]
                at += 1
            else:
                g_im[b][b] = jnp.zeros_like(sums[0])
    g = (
        jnp.stack([jnp.stack(row) for row in g_re]),
        jnp.stack([jnp.stack(row) for row in g_im]),
    )
    turn = phase_table(offsets, bins, frames)
    both = cmul((turn[0][:, None], -turn[1][:, None]), (turn[0][None], turn[1][None]))
    basis, energy = leading_basis(cmul(both, g))
    live = jnp.arange(MODES, dtype=jnp.int32)[:, None] < modes_kept[None, :]
    factor = live.astype(jnp.float32) / jnp.sqrt(energy)
    modes = []
    for m in range(MODES):
        q = cmul(turn, basis[m])
        q = (q[0] * factor[m], q[1] * factor[m])
        re = jnp.sum(u[0] * q[0][:, None] - u[1] * q[1][:, None], axis=0)
        im = jnp.sum(u[0] * q[1][:, None] + u[1] * q[0][:, None], axis=0)
        modes.append(jnp.stack([re, im]))
    return energy, jnp.stack(modes)


CHUNKS = (4, 4)


def swap_with(values, step):
    ranks = lax.axis_size("freq")
    return lax.ppermute(values, "freq", [(i, i ^ step) for i in range(ranks)])


def tiled(signal, offsets, pairing, modes_kept):
    rows, blocks, points = signal.shape
    ranks = lax.axis_size("freq")
    rank = lax.axis_index("freq")
    bins = rows * ranks // 2
    core = (rank & 1).reshape(1)
    turn = phase_table(offsets, bins, rows * ranks)
    tables = [jnp.asarray(t) for t in split_table(rows * ranks)]
    got, first = [], 0
    for count in CHUNKS:
        part = pack(signal, pairing, first, count)
        signal, part = lax.optimization_barrier((signal, part))
        got.append(lax.all_to_all(part, "freq", split_axis=0, concat_axis=0, tiled=True))
        first += count
    parts, gram = [], None
    for n, x in enumerate(got):
        final = n == len(got) - 1
        re, im, *grams = spectra(blocks, x.reshape(rows * ranks, -1), tables, core, parts, gram, final)
        parts.append((re, im))
        gram = grams[0]
    mine = gram + swap_with(grams[1], 1)
    step = 2
    while step < ranks:
        mine = mine + swap_with(mine, step)
        step *= 2
    other = swap_with(mine, 1)
    energy, modes = finish(blocks, points, core, mine, other, turn, modes_kept, parts)
    return energy, modes


def local(signal, offsets, pairing, modes_kept):
    rows, blocks, points = signal.shape
    ranks = lax.axis_size("freq")
    rank = lax.axis_index("freq")
    bins = rows * ranks // 2
    fits = points == ranks * LANES and rows % 16 == 0 and ranks >= GROUP and ranks & (ranks - 1) == 0
    fits = fits and bins % (2 * LANES) == 0 and blocks == sum(CHUNKS) == 8
    energy, modes = (tiled if fits else plain)(signal, offsets, pairing, modes_kept)
    modes = modes.reshape(MODES, 2, 2, points // ranks // 2, bins)
    held = lax.dynamic_slice_in_dim(energy, rank * (bins // ranks), bins // ranks, axis=1)
    return held.T, modes.transpose(4, 0, 1, 2, 3)


def solution(mesh):
    placed = (P("freq", None, "groups"), P(), P("groups"), P())
    return jax.shard_map(
        local,
        mesh=mesh,
        in_specs=placed,
        out_specs=(P("freq", "groups"), P(None, None, None, None, ("groups", "freq"))),
        check_vma=False,
    )
```

```python
import math

import jax
import jax.numpy as jnp
import ml_dtypes
import numpy as np
from jax import lax
from jax.experimental import pallas as pl
from jax.experimental.pallas import tpu as pltpu
from jax.sharding import PartitionSpec as P

MODES = 4
ITERS = 3
precise = lax.Precision.HIGHEST


def transform_table(frames):
    steps = np.arange(frames)
    shape = 0.5 - 0.5 * np.cos(2.0 * np.pi * steps / frames)
    window = shape / np.sqrt(np.sum(shape * shape))
    phase = (steps[:, None] * np.arange(frames // 2)[None, :] % frames) * (2.0 * np.pi / frames)
    table = np.concatenate([np.cos(phase), -np.sin(phase)], axis=1) * window[:, None]
    return table.astype(np.float32)


def phase_table(offsets, bins, frames):
    steps = jnp.arange(bins, dtype=jnp.int32)[None, :] * offsets[:, None] % frames
    angle = steps.astype(jnp.float32) * (2.0 * math.pi / frames)
    return jnp.cos(angle), -jnp.sin(angle)


def sum_over(values, axis):
    size = lax.axis_size(axis)
    if size & (size - 1):
        return lax.psum(values, axis)
    step = 1
    while step < size:
        values = values + lax.ppermute(values, axis, [(i, i ^ step) for i in range(size)])
        step *= 2
    return values


def cmul(a, b):
    return a[0] * b[0] - a[1] * b[1], a[0] * b[1] + a[1] * b[0]


def cdot(a, b):
    return (
        jnp.sum(a[0] * b[0] + a[1] * b[1], axis=0, keepdims=True),
        jnp.sum(a[0] * b[1] - a[1] * b[0], axis=0, keepdims=True),
    )


def times_gram(g, v):
    re = jnp.sum(g[0] * v[0][None] - g[1] * v[1][None], axis=1)
    im = jnp.sum(g[0] * v[1][None] + g[1] * v[0][None], axis=1)
    return re, im


def leading_basis(g):
    blocks, bins = g[0].shape[0], g[0].shape[-1]
    ys = [(g[0][:, m], g[1][:, m]) for m in range(MODES)]
    for sweep in range(ITERS):
        done = []
        for v in ys:
            for q in done:
                part = cmul(cdot(q, v), q)
                v = (v[0] - part[0], v[1] - part[1])
            length = jnp.sqrt(jnp.sum(v[0] * v[0] + v[1] * v[1], axis=0, keepdims=True))
            done.append((v[0] / length, v[1] / length))
        ys = [times_gram(g, q) for q in done]
    energy = jnp.concatenate([cdot(q, y)[0] for q, y in zip(done, ys)], axis=0)
    return done, energy


LANES = 128
GROUP = 4
VMEM = pltpu.CompilerParams(vmem_limit_bytes=60 * 2**20)
SMALL = pltpu.CompilerParams(vmem_limit_bytes=50 * 2**20)


def split_table(frames):
    table = transform_table(frames).reshape(frames, 2, -1, LANES)
    table = table.transpose(0, 2, 1, 3).reshape(frames, frames)
    high = table.astype(ml_dtypes.bfloat16)
    low = (table - high.astype(np.float32)).astype(ml_dtypes.bfloat16)
    return high, low


def two_terms(x):
    high = x.astype(jnp.bfloat16)
    return high, (x - high.astype(jnp.float32)).astype(jnp.bfloat16)


def three_terms(x):
    high, rest = x.astype(jnp.bfloat16), None
    rest = x - high.astype(jnp.float32)
    mid = rest.astype(jnp.bfloat16)
    return high, mid, (rest - mid.astype(jnp.float32)).astype(jnp.bfloat16)


def dot(a, b):
    return jnp.dot(a, b, preferred_element_type=jnp.float32)


def in_hbm(arrays):
    return [pltpu.with_memory_space_constraint(a, pltpu.HBM) for a in arrays]


def pack_kernel(blocks, first, count, strips, *refs):
    signals, pairing, out, one_row, low_pick, total = refs[:strips], *refs[strips:]
    step = pl.program_id(0)
    rows = signals[0].shape[0] // blocks
    ranks = out.shape[0]
    depth = strips * LANES

    @pl.when(step == 0)
    def _():
        place = lax.broadcasted_iota(jnp.int32, (LANES, LANES), 1)
        source = lax.broadcasted_iota(jnp.int32, (LANES, LANES), 0)
        half = LANES // 2
        wanted = jnp.where(place < half, 2 * place, 2 * (place - half) + 1)
        turn = (wanted == source).astype(jnp.float32).astype(jnp.bfloat16)
        lines = pairing[...]
        upper = (lines >> 5).astype(jnp.float32).astype(jnp.bfloat16)
        lower = (lines & 31).astype(jnp.float32).astype(jnp.bfloat16)
        one_row[...] = (dot(upper, turn) * 32.0 + dot(lower, turn)).astype(jnp.int32)
        total[...] = jnp.zeros_like(total)
        for n in range(ranks):
            low_pick[:, n * LANES : (n + 1) * LANES] = jnp.where(
                source == one_row[n : n + 1, :] % LANES, 1.0, 0.0
            ).astype(jnp.bfloat16)

    x = jnp.concatenate(
        [
            jnp.concatenate([strip[pl.ds(b, rows, stride=blocks), :] for strip in signals], axis=1)
            for b in range(first, first + count)
        ],
        axis=0,
    )
    stacked = jnp.concatenate(three_terms(x), axis=0)
    third = stacked.shape[0] // 3
    here = [
        jnp.where(one_row[...] // LANES == step * strips + n, 1.0, 0.0) for n in range(strips)
    ]
    for at in range(0, ranks, GROUP):
        pick = []
        for n in range(at, at + GROUP):
            spot = low_pick[:, n * LANES : (n + 1) * LANES]
            strip = [
                spot * jnp.broadcast_to(line[n : n + 1], spot.shape).astype(jnp.bfloat16) for line in here
            ]
            pick.append(jnp.concatenate(strip, axis=0))
        got = dot(stacked, jnp.concatenate(pick, axis=1))
        spot = (slice(None), slice(at * LANES, (at + GROUP) * LANES))
        total[spot] += got[:third] + got[third : 2 * third] + got[2 * third :]

    @pl.when(step == pl.num_programs(0) - 1)
    def _():
        for n in range(ranks):
            for b in range(count):
                out[n, :, b * LANES : (b + 1) * LANES] = total[
                    b * rows : (b + 1) * rows, n * LANES : (n + 1) * LANES
                ]


def pack(signal, pairing, first, count):
    rows, blocks, points = signal.shape
    strips = 4
    ranks = points // LANES
    shape = (ranks, rows, count * LANES)
    return pl.pallas_call(
        lambda *refs: pack_kernel(blocks, first, count, strips, *refs),
        grid=(points // (strips * LANES),),
        in_specs=[
            pl.BlockSpec((rows * blocks, LANES), lambda i, n=n: (0, strips * i + n))
            for n in range(strips)
        ]
        + [pl.BlockSpec((ranks, LANES), lambda i: (0, 0))],
        out_specs=pl.BlockSpec(shape, lambda i: (0, 0, 0)),
        scratch_shapes=[
            pltpu.VMEM((ranks, LANES), jnp.int32),
            pltpu.VMEM((LANES, points), jnp.bfloat16),
            pltpu.VMEM((rows * count, points), jnp.float32),
        ],
        out_shape=jax.ShapeDtypeStruct(shape, jnp.float32),
        compiler_params=VMEM,
        cost_estimate=pl.CostEstimate(
            flops=6 * rows * count * points * points, bytes_accessed=8 * 2**20, transcendentals=0
        ),
    )(*[signal.reshape(rows * blocks, points)] * strips, pairing.reshape(-1, LANES))


def pair_list(blocks):
    return [(b, e) for b in range(blocks) for e in range(b, blocks)]


def gram_tile(parts, blocks, gram):
    where = []
    for re, im in parts:
        where += [(re, im, n * LANES) for n in range(re.shape[0] // LANES)]
    fresh = len(where)
    start = fresh - parts[-1][0].shape[0] // LANES
    todo = [(b, e) for e in range(start, fresh) for b in range(e + 1)]
    most = 14
    for first in range(0, len(todo), most):
        chunk = todo[first : first + most]
        used = sorted({b for b, _ in chunk} | {e for _, e in chunk})

        def body(i, sums):
            spot = pl.multiple_of(i * 8, 8)
            u = {}
            for b in used:
                re, im, base = where[b]
                u[b] = (re[pl.ds(base + spot, 8), :], im[pl.ds(base + spot, 8), :])
            out = []
            for b, e in chunk:
                (br, bi), (er, ei) = u[b], u[e]
                out.append(br * er + bi * ei)
                if b != e:
                    out.append(br * ei - bi * er)
            return tuple(s + o for s, o in zip(sums, out))

        rows = []
        for b, e in chunk:
            rows += [e * blocks + b] if b == e else [e * blocks + b, b * blocks + e]
        zero = jnp.zeros((8, gram.shape[1]), jnp.float32)
        sums = lax.fori_loop(0, LANES // 8, body, (zero,) * len(rows))
        for row, value in zip(rows, sums):
            gram[row : row + 1, :] = jnp.sum(value, axis=0, keepdims=True)


def spectra_kernel(blocks, others, final, core, x, high, low, *refs):
    parts = [(refs[2 * n], refs[2 * n + 1]) for n in range(others)]
    refs = refs[2 * others :]
    before, refs = (refs[0], refs[1:]) if others else (None, refs)
    (re, im), grams, (x_high, x_low, gram) = refs[:2], refs[2:-3], refs[-3:]
    step = pl.program_id(0)

    @pl.when(step == 0)
    def _():
        x_high[...], x_low[...] = two_terms(x[...].T)

    got = dot(x_high[...], high[...]) + dot(x_low[...], high[...]) + dot(x_high[...], low[...])
    re[...] = got[:, :LANES]
    im[...] = got[:, LANES:]
    gram[...] = before[...] if others else jnp.zeros_like(gram)
    gram_tile(parts + [(re, im)], blocks, gram)
    if final:
        half = step // (pl.num_programs(0) // 2)
        lane = pl.multiple_of(step % (pl.num_programs(0) // 2) * LANES, LANES)

        @pl.when(half == core[0])
        def _():
            grams[0][:, pl.ds(lane, LANES)] = gram[...]

        @pl.when(half != core[0])
        def _():
            grams[1][:, pl.ds(lane, LANES)] = gram[...]
    else:
        grams[0][...] = gram[...]


def spectra(blocks, x, tables, core, others=(), before=None, final=False):
    frames, width = x.shape
    bins = frames // 2
    held = pl.BlockSpec((width, LANES), lambda i, c: (0, i))
    shape = pltpu.HBM((width, bins), jnp.float32)
    flat = [a for part in others for a in part] + ([before] if others else [])
    in_specs = [pl.BlockSpec((frames, width), lambda i, c: (0, 0))]
    in_specs += [pl.BlockSpec((frames, 2 * LANES), lambda i, c: (0, i))] * 2
    in_specs += [pl.BlockSpec((a.shape[0], LANES), lambda i, c: (0, i)) for a in flat]
    square = blocks * blocks
    if final:
        out_specs = [held] * 2 + [pl.BlockSpec((square, bins // 2), lambda i, c: (0, 0))] * 2
        out_shape = [shape] * 2 + [jax.ShapeDtypeStruct((square, bins // 2), jnp.float32)] * 2
    else:
        out_specs = [held] * 2 + [pl.BlockSpec((square, LANES), lambda i, c: (0, i))]
        out_shape = [shape] * 2 + [jax.ShapeDtypeStruct((square, bins), jnp.float32)]
    return pl.pallas_call(
        lambda *refs: spectra_kernel(blocks, len(others), final, *refs),
        grid_spec=pltpu.PrefetchScalarGridSpec(
            num_scalar_prefetch=1,
            grid=(bins // LANES,),
            in_specs=in_specs,
            out_specs=out_specs,
            scratch_shapes=[pltpu.VMEM((width, frames), jnp.bfloat16)] * 2
            + [pltpu.VMEM((square, LANES), jnp.float32)],
        ),
        out_shape=out_shape,
        compiler_params=SMALL,
        cost_estimate=pl.CostEstimate(
            flops=6 * width * frames * frames, bytes_accessed=12 * 2**20, transcendentals=0
        ),
    )(core, x, *in_hbm([*tables, *flat]))


def row_dot(a, b):
    return (
        jnp.sum(a[0] * b[0] + a[1] * b[1], axis=0, keepdims=True),
        jnp.sum(a[0] * b[1] - a[1] * b[0], axis=0, keepdims=True),
    )


def finish_kernel(blocks, points, parts, core, mine, other, turn_re, turn_im, kept, *refs):
    spectra_refs = [(refs[2 * n], refs[2 * n + 1]) for n in range(parts)]
    energy, modes, tiles, basis = refs[2 * parts :]
    step = pl.program_id(0)

    @pl.when(step == 0)
    def _():
        swap = core[0] == 1
        half = mine.shape[1]
        count = 2 * half // LANES
        for t in range(count):
            lane = slice(t * LANES % half, t * LANES % half + LANES)
            ours = jnp.logical_xor(swap, t * LANES >= half)
            tiles[t] = jnp.where(ours, other[:, lane], mine[:, lane]) * (1.0 / points)
        ph = (turn_re[...], turn_im[...])
        back = (ph[0], -ph[1])
        row = lax.broadcasted_iota(jnp.int32, ph[0].shape, 0)
        g = []
        for e in range(blocks):
            down = [tiles[t, e * blocks : (e + 1) * blocks, :] for t in range(count)]
            across = [tiles[t, pl.ds(e, blocks, stride=blocks), :] for t in range(count)]
            down, across = jnp.concatenate(down, axis=1), jnp.concatenate(across, axis=1)
            re = jnp.where(row <= e, down, across)
            im = jnp.where(row < e, across, jnp.where(row > e, -down, 0.0))
            column = (ph[0][e : e + 1], ph[1][e : e + 1])
            g.append(cmul(cmul(back, (re, im)), column))
        ys = g[:MODES]
        for sweep in range(ITERS):
            done = []
            for v in ys:
                for q in done:
                    part = cmul(row_dot(q, v), q)
                    v = (v[0] - part[0], v[1] - part[1])
                length = jnp.sqrt(jnp.sum(v[0] * v[0] + v[1] * v[1], axis=0, keepdims=True))
                done.append((v[0] / length, v[1] / length))
            ys = []
            for q in done:
                re, im = jnp.zeros_like(q[0]), jnp.zeros_like(q[0])
                for e in range(blocks):
                    part = cmul(g[e], (q[0][e : e + 1], q[1][e : e + 1]))
                    re, im = re + part[0], im + part[1]
                ys.append((re, im))
        for m, (q, y) in enumerate(zip(done, ys)):
            level = row_dot(q, y)[0]
            energy[m : m + 1, :] = level
            factor = jnp.where(kept[...] > m, 1.0, 0.0) / jnp.sqrt(level)
            re, im = cmul(ph, q)
            re, im = re * factor, im * factor
            for t in range(count):
                lane = slice(t * LANES, (t + 1) * LANES)
                basis[t, 2 * m * blocks : (2 * m + 1) * blocks, :] = re[:, lane]
                basis[t, (2 * m + 1) * blocks : (2 * m + 2) * blocks, :] = im[:, lane]

    where = []
    for re, im in spectra_refs:
        where += [(re, im, n * LANES) for n in range(re.shape[0] // LANES)]
    for m in range(MODES):
        total_re, total_im = None, None
        for b, (re, im, base) in enumerate(where):
            u = (re[base : base + LANES, :], im[base : base + LANES, :])
            q = [basis[step, pl.ds((2 * m + n) * blocks + b, 1), :] for n in (0, 1)]
            part = cmul(u, q)
            total_re = part[0] if b == 0 else total_re + part[0]
            total_im = part[1] if b == 0 else total_im + part[1]
        modes[m, 0] = total_re
        modes[m, 1] = total_im


def finish(blocks, points, core, mine, other, turn, kept, parts):
    square, half = mine.shape
    bins = 2 * half
    flat = [a for part in parts for a in part]
    whole = lambda a: pl.BlockSpec(a.shape, lambda i, c: (0, 0))
    kept = kept.reshape(1, bins)
    small = [mine, other, *turn, kept]
    return pl.pallas_call(
        lambda *refs: finish_kernel(blocks, points, len(parts), *refs),
        grid_spec=pltpu.PrefetchScalarGridSpec(
            num_scalar_prefetch=1,
            grid=(bins // LANES,),
            in_specs=[whole(a) for a in small]
            + [pl.BlockSpec((a.shape[0], LANES), lambda i, c: (0, i)) for a in flat],
            out_specs=[
                pl.BlockSpec((MODES, bins), lambda i, c: (0, 0)),
                pl.BlockSpec((MODES, 2, LANES, LANES), lambda i, c: (0, 0, 0, i)),
            ],
            scratch_shapes=[
                pltpu.VMEM((bins // LANES, square, LANES), jnp.float32),
                pltpu.VMEM((bins // LANES, 2 * MODES * blocks, LANES), jnp.float32),
            ],
        ),
        out_shape=[
            jax.ShapeDtypeStruct((MODES, bins), jnp.float32),
            jax.ShapeDtypeStruct((MODES, 2, LANES, bins), jnp.float32),
        ],
        compiler_params=SMALL,
        cost_estimate=pl.CostEstimate(
            flops=16 * MODES * blocks * LANES * bins, bytes_accessed=6 * 2**20, transcendentals=0
        ),
    )(core, *small, *in_hbm(flat))


def gram_of(u, blocks):
    pairs = []
    for b, e in pair_list(blocks):
        pairs.append(jnp.sum(u[0][b] * u[0][e] + u[1][b] * u[1][e], axis=0))
        if e > b:
            pairs.append(jnp.sum(u[0][b] * u[1][e] - u[1][b] * u[0][e], axis=0))
    return jnp.stack(pairs, axis=0)


def plain(signal, offsets, pairing, modes_kept):
    rows, blocks, points = signal.shape
    ranks = lax.axis_size("freq")
    rank = lax.axis_index("freq")
    frames = rows * ranks
    bins = frames // 2
    own = points // ranks
    order = pairing.reshape(ranks, own // 2, 2).transpose(0, 2, 1).reshape(-1)
    packed = jnp.take(signal, order, axis=2).reshape(rows, blocks, ranks, own)
    packed = packed.transpose(2, 0, 1, 3)
    series = lax.all_to_all(packed, "freq", split_axis=0, concat_axis=0, tiled=True)
    series = series.reshape(frames, blocks * own)
    table = jnp.asarray(transform_table(frames))
    spectra = lax.dot_general(series, table, (((0,), (0,)), ((), ())), precision=precise)
    spectra = spectra.reshape(blocks, own, 2, bins)
    u = (spectra[:, :, 0], spectra[:, :, 1])
    sums = sum_over(gram_of(u, blocks), "freq") * (1.0 / points)
    g_re = [[None] * blocks for _ in range(blocks)]
    g_im = [[None] * blocks for _ in range(blocks)]
    at = 0
    for b in range(blocks):
        for e in range(b, blocks):
            g_re[b][e] = g_re[e][b] = sums[at]
            at += 1
            if e > b:
                g_im[b][e], g_im[e][b] = sums[at], -sums[at]
                at += 1
            else:
                g_im[b][b] = jnp.zeros_like(sums[0])
    g = (
        jnp.stack([jnp.stack(row) for row in g_re]),
        jnp.stack([jnp.stack(row) for row in g_im]),
    )
    turn = phase_table(offsets, bins, frames)
    both = cmul((turn[0][:, None], -turn[1][:, None]), (turn[0][None], turn[1][None]))
    basis, energy = leading_basis(cmul(both, g))
    live = jnp.arange(MODES, dtype=jnp.int32)[:, None] < modes_kept[None, :]
    factor = live.astype(jnp.float32) / jnp.sqrt(energy)
    modes = []
    for m in range(MODES):
        q = cmul(turn, basis[m])
        q = (q[0] * factor[m], q[1] * factor[m])
        re = jnp.sum(u[0] * q[0][:, None] - u[1] * q[1][:, None], axis=0)
        im = jnp.sum(u[0] * q[1][:, None] + u[1] * q[0][:, None], axis=0)
        modes.append(jnp.stack([re, im]))
    return energy, jnp.stack(modes)


CHUNKS = (4, 4)


def swap_with(values, step):
    ranks = lax.axis_size("freq")
    return lax.ppermute(values, "freq", [(i, i ^ step) for i in range(ranks)])


def tiled(signal, offsets, pairing, modes_kept):
    rows, blocks, points = signal.shape
    ranks = lax.axis_size("freq")
    rank = lax.axis_index("freq")
    bins = rows * ranks // 2
    core = (rank & 1).reshape(1)
    turn = phase_table(offsets, bins, rows * ranks)
    tables = [jnp.asarray(t) for t in split_table(rows * ranks)]
    got, first = [], 0
    for count in CHUNKS:
        part = pack(signal, pairing, first, count)
        signal, part = lax.optimization_barrier((signal, part))
        got.append(lax.all_to_all(part, "freq", split_axis=0, concat_axis=0, tiled=True))
        first += count
    parts, gram = [], None
    for n, x in enumerate(got):
        final = n == len(got) - 1
        re, im, *grams = spectra(blocks, x.reshape(rows * ranks, -1), tables, core, parts, gram, final)
        parts.append((re, im))
        gram = grams[0]
    mine = gram + swap_with(grams[1], 1)
    step = 2
    while step < ranks:
        mine = mine + swap_with(mine, step)
        step *= 2
    other = swap_with(mine, 1)
    energy, modes = finish(blocks, points, core, mine, other, turn, modes_kept, parts)
    return energy, modes


def local(signal, offsets, pairing, modes_kept):
    rows, blocks, points = signal.shape
    ranks = lax.axis_size("freq")
    rank = lax.axis_index("freq")
    bins = rows * ranks // 2
    fits = points == ranks * LANES and rows % 16 == 0 and ranks >= GROUP and ranks & (ranks - 1) == 0
    fits = fits and bins % (2 * LANES) == 0 and blocks == sum(CHUNKS) == 8
    energy, modes = (tiled if fits else plain)(signal, offsets, pairing, modes_kept)
    modes = modes.reshape(MODES, 2, 2, points // ranks // 2, bins)
    held = lax.dynamic_slice_in_dim(energy, rank * (bins // ranks), bins // ranks, axis=1)
    return held.T, modes.transpose(4, 0, 1, 2, 3)


def solution(mesh):
    placed = (P("freq", None, "groups"), P(), P("groups"), P())
    return jax.shard_map(
        local,
        mesh=mesh,
        in_specs=placed,
        out_specs=(P("freq", "groups"), P(None, None, None, None, ("groups", "freq"))),
        check_vma=False,
    )
```

```python
import math

import jax
import jax.numpy as jnp
import ml_dtypes
import numpy as np
from jax import lax
from jax.experimental import pallas as pl
from jax.experimental.pallas import tpu as pltpu
from jax.sharding import PartitionSpec as P

MODES = 4
ITERS = 3
precise = lax.Precision.HIGHEST


def transform_table(frames):
    steps = np.arange(frames)
    shape = 0.5 - 0.5 * np.cos(2.0 * np.pi * steps / frames)
    window = shape / np.sqrt(np.sum(shape * shape))
    phase = (steps[:, None] * np.arange(frames // 2)[None, :] % frames) * (2.0 * np.pi / frames)
    table = np.concatenate([np.cos(phase), -np.sin(phase)], axis=1) * window[:, None]
    return table.astype(np.float32)


def phase_table(offsets, bins, frames):
    steps = jnp.arange(bins, dtype=jnp.int32)[None, :] * offsets[:, None] % frames
    angle = steps.astype(jnp.float32) * (2.0 * math.pi / frames)
    return jnp.cos(angle), -jnp.sin(angle)


def sum_over(values, axis):
    size = lax.axis_size(axis)
    if size & (size - 1):
        return lax.psum(values, axis)
    step = 1
    while step < size:
        values = values + lax.ppermute(values, axis, [(i, i ^ step) for i in range(size)])
        step *= 2
    return values


def cmul(a, b):
    return a[0] * b[0] - a[1] * b[1], a[0] * b[1] + a[1] * b[0]


def cdot(a, b):
    return (
        jnp.sum(a[0] * b[0] + a[1] * b[1], axis=0, keepdims=True),
        jnp.sum(a[0] * b[1] - a[1] * b[0], axis=0, keepdims=True),
    )


def times_gram(g, v):
    re = jnp.sum(g[0] * v[0][None] - g[1] * v[1][None], axis=1)
    im = jnp.sum(g[0] * v[1][None] + g[1] * v[0][None], axis=1)
    return re, im


def leading_basis(g):
    blocks, bins = g[0].shape[0], g[0].shape[-1]
    ys = [(g[0][:, m], g[1][:, m]) for m in range(MODES)]
    for sweep in range(ITERS):
        done = []
        for v in ys:
            for q in done:
                part = cmul(cdot(q, v), q)
                v = (v[0] - part[0], v[1] - part[1])
            length = jnp.sqrt(jnp.sum(v[0] * v[0] + v[1] * v[1], axis=0, keepdims=True))
            done.append((v[0] / length, v[1] / length))
        ys = [times_gram(g, q) for q in done]
    energy = jnp.concatenate([cdot(q, y)[0] for q, y in zip(done, ys)], axis=0)
    return done, energy


LANES = 128
GROUP = 4
VMEM = pltpu.CompilerParams(vmem_limit_bytes=60 * 2**20)
SMALL = pltpu.CompilerParams(vmem_limit_bytes=50 * 2**20)


def split_table(frames):
    table = transform_table(frames).reshape(frames, 2, -1, LANES)
    table = table.transpose(0, 2, 1, 3).reshape(frames, frames)
    high = table.astype(ml_dtypes.bfloat16)
    low = (table - high.astype(np.float32)).astype(ml_dtypes.bfloat16)
    return high, low


def two_terms(x):
    high = x.astype(jnp.bfloat16)
    return high, (x - high.astype(jnp.float32)).astype(jnp.bfloat16)


def three_terms(x):
    high, rest = x.astype(jnp.bfloat16), None
    rest = x - high.astype(jnp.float32)
    mid = rest.astype(jnp.bfloat16)
    return high, mid, (rest - mid.astype(jnp.float32)).astype(jnp.bfloat16)


def dot(a, b):
    return jnp.dot(a, b, preferred_element_type=jnp.float32)


def in_hbm(arrays):
    return [pltpu.with_memory_space_constraint(a, pltpu.HBM) for a in arrays]


def pack_kernel(blocks, first, count, strips, *refs):
    signals, pairing, out, one_row, low_pick, total = refs[:strips], *refs[strips:]
    step = pl.program_id(0)
    rows = signals[0].shape[0] // blocks
    ranks = out.shape[0]
    depth = strips * LANES

    @pl.when(step == 0)
    def _():
        place = lax.broadcasted_iota(jnp.int32, (LANES, LANES), 1)
        source = lax.broadcasted_iota(jnp.int32, (LANES, LANES), 0)
        half = LANES // 2
        wanted = jnp.where(place < half, 2 * place, 2 * (place - half) + 1)
        turn = (wanted == source).astype(jnp.float32).astype(jnp.bfloat16)
        lines = pairing[...]
        upper = (lines >> 5).astype(jnp.float32).astype(jnp.bfloat16)
        lower = (lines & 31).astype(jnp.float32).astype(jnp.bfloat16)
        one_row[...] = (dot(upper, turn) * 32.0 + dot(lower, turn)).astype(jnp.int32)
        total[...] = jnp.zeros_like(total)
        for n in range(ranks):
            low_pick[:, n * LANES : (n + 1) * LANES] = jnp.where(
                source == one_row[n : n + 1, :] % LANES, 1.0, 0.0
            ).astype(jnp.bfloat16)

    x = jnp.concatenate(
        [
            jnp.concatenate([strip[pl.ds(b, rows, stride=blocks), :] for strip in signals], axis=1)
            for b in range(first, first + count)
        ],
        axis=0,
    )
    stacked = jnp.concatenate(three_terms(x), axis=0)
    third = stacked.shape[0] // 3
    here = [
        jnp.where(one_row[...] // LANES == step * strips + n, 1.0, 0.0) for n in range(strips)
    ]
    for at in range(0, ranks, GROUP):
        pick = []
        for n in range(at, at + GROUP):
            spot = low_pick[:, n * LANES : (n + 1) * LANES]
            strip = [
                spot * jnp.broadcast_to(line[n : n + 1], spot.shape).astype(jnp.bfloat16) for line in here
            ]
            pick.append(jnp.concatenate(strip, axis=0))
        got = dot(stacked, jnp.concatenate(pick, axis=1))
        spot = (slice(None), slice(at * LANES, (at + GROUP) * LANES))
        total[spot] += got[:third] + got[third : 2 * third] + got[2 * third :]

    @pl.when(step == pl.num_programs(0) - 1)
    def _():
        for n in range(ranks):
            for b in range(count):
                out[n, :, b * LANES : (b + 1) * LANES] = total[
                    b * rows : (b + 1) * rows, n * LANES : (n + 1) * LANES
                ]


def pack(signal, pairing, first, count):
    rows, blocks, points = signal.shape
    strips = 4
    ranks = points // LANES
    shape = (ranks, rows, count * LANES)
    return pl.pallas_call(
        lambda *refs: pack_kernel(blocks, first, count, strips, *refs),
        grid=(points // (strips * LANES),),
        in_specs=[
            pl.BlockSpec((rows * blocks, LANES), lambda i, n=n: (0, strips * i + n))
            for n in range(strips)
        ]
        + [pl.BlockSpec((ranks, LANES), lambda i: (0, 0))],
        out_specs=pl.BlockSpec(shape, lambda i: (0, 0, 0)),
        scratch_shapes=[
            pltpu.VMEM((ranks, LANES), jnp.int32),
            pltpu.VMEM((LANES, points), jnp.bfloat16),
            pltpu.VMEM((rows * count, points), jnp.float32),
        ],
        out_shape=jax.ShapeDtypeStruct(shape, jnp.float32),
        compiler_params=VMEM,
        cost_estimate=pl.CostEstimate(
            flops=6 * rows * count * points * points, bytes_accessed=8 * 2**20, transcendentals=0
        ),
    )(*[signal.reshape(rows * blocks, points)] * strips, pairing.reshape(-1, LANES))


def pair_list(blocks):
    return [(b, e) for b in range(blocks) for e in range(b, blocks)]


def gram_tile(parts, blocks, gram):
    where = []
    for re, im in parts:
        where += [(re, im, n * LANES) for n in range(re.shape[0] // LANES)]
    fresh = len(where)
    start = fresh - parts[-1][0].shape[0] // LANES
    todo = [(b, e) for e in range(start, fresh) for b in range(e + 1)]
    most = 14
    for first in range(0, len(todo), most):
        chunk = todo[first : first + most]
        used = sorted({b for b, _ in chunk} | {e for _, e in chunk})

        def body(i, sums):
            spot = pl.multiple_of(i * 8, 8)
            u = {}
            for b in used:
                re, im, base = where[b]
                u[b] = (re[pl.ds(base + spot, 8), :], im[pl.ds(base + spot, 8), :])
            out = []
            for b, e in chunk:
                (br, bi), (er, ei) = u[b], u[e]
                out.append(br * er + bi * ei)
                if b != e:
                    out.append(br * ei - bi * er)
            return tuple(s + o for s, o in zip(sums, out))

        rows = []
        for b, e in chunk:
            rows += [e * blocks + b] if b == e else [e * blocks + b, b * blocks + e]
        zero = jnp.zeros((8, gram.shape[1]), jnp.float32)
        sums = lax.fori_loop(0, LANES // 8, body, (zero,) * len(rows), unroll=True)
        for row, value in zip(rows, sums):
            gram[row : row + 1, :] = jnp.sum(value, axis=0, keepdims=True)


def spectra_kernel(blocks, others, final, core, x, high, low, *refs):
    parts = [(refs[2 * n], refs[2 * n + 1]) for n in range(others)]
    refs = refs[2 * others :]
    before, refs = (refs[0], refs[1:]) if others else (None, refs)
    (re, im), grams, (x_high, x_low, gram) = refs[:2], refs[2:-3], refs[-3:]
    step = pl.program_id(0)

    def put(got):
        re[...] = got[:, :LANES]
        im[...] = got[:, LANES:]

    @pl.when(step == 0)
    def _():
        depth = 2 * LANES
        got = None
        for at in range(0, x.shape[0], depth):
            spot = (slice(None), slice(at, at + depth))
            x_high[spot], x_low[spot] = terms = two_terms(x[at : at + depth, :].T)
            w = (high[at : at + depth, :], low[at : at + depth, :])
            part = dot(terms[0], w[0]) + dot(terms[1], w[0]) + dot(terms[0], w[1])
            got = part if at == 0 else got + part
        put(got)

    @pl.when(step > 0)
    def _():
        put(dot(x_high[...], high[...]) + dot(x_low[...], high[...]) + dot(x_high[...], low[...]))

    gram[...] = before[...] if others else jnp.zeros_like(gram)
    gram_tile(parts + [(re, im)], blocks, gram)
    if final:
        half = step // (pl.num_programs(0) // 2)
        lane = pl.multiple_of(step % (pl.num_programs(0) // 2) * LANES, LANES)

        @pl.when(half == core[0])
        def _():
            grams[0][:, pl.ds(lane, LANES)] = gram[...]

        @pl.when(half != core[0])
        def _():
            grams[1][:, pl.ds(lane, LANES)] = gram[...]
    else:
        grams[0][...] = gram[...]


def spectra(blocks, x, tables, core, others=(), before=None, final=False):
    frames, width = x.shape
    bins = frames // 2
    held = pl.BlockSpec((width, LANES), lambda i, c: (0, i))
    shape = pltpu.HBM((width, bins), jnp.float32)
    flat = [a for part in others for a in part] + ([before] if others else [])
    in_specs = [pl.BlockSpec(memory_space=pltpu.VMEM)]
    in_specs += [pl.BlockSpec((frames, 2 * LANES), lambda i, c: (0, i))] * 2
    in_specs += [pl.BlockSpec((a.shape[0], LANES), lambda i, c: (0, i)) for a in flat]
    square = blocks * blocks
    if final:
        out_specs = [held] * 2 + [pl.BlockSpec((square, bins // 2), lambda i, c: (0, 0))] * 2
        out_shape = [shape] * 2 + [jax.ShapeDtypeStruct((square, bins // 2), jnp.float32)] * 2
    else:
        out_specs = [held] * 2 + [pl.BlockSpec((square, LANES), lambda i, c: (0, i))]
        out_shape = [shape] * 2 + [jax.ShapeDtypeStruct((square, bins), jnp.float32)]
    return pl.pallas_call(
        lambda *refs: spectra_kernel(blocks, len(others), final, *refs),
        grid_spec=pltpu.PrefetchScalarGridSpec(
            num_scalar_prefetch=1,
            grid=(bins // LANES,),
            in_specs=in_specs,
            out_specs=out_specs,
            scratch_shapes=[pltpu.VMEM((width, frames), jnp.bfloat16)] * 2
            + [pltpu.VMEM((square, LANES), jnp.float32)],
        ),
        out_shape=out_shape,
        compiler_params=SMALL,
        cost_estimate=pl.CostEstimate(
            flops=6 * width * frames * frames, bytes_accessed=12 * 2**20, transcendentals=0
        ),
    )(core, x, *in_hbm([*tables, *flat]))


def row_dot(a, b):
    return (
        jnp.sum(a[0] * b[0] + a[1] * b[1], axis=0, keepdims=True),
        jnp.sum(a[0] * b[1] - a[1] * b[0], axis=0, keepdims=True),
    )


def finish_kernel(blocks, points, parts, core, mine, other, turn_re, turn_im, kept, *refs):
    spectra_refs = [(refs[2 * n], refs[2 * n + 1]) for n in range(parts)]
    energy, modes, tiles, basis, levels = refs[2 * parts :]
    step = pl.program_id(0)

    @pl.when(step == 0)
    def _():
        swap = core[0] == 1
        half = mine.shape[1]
        count = 2 * half // LANES
        for t in range(count):
            lane = slice(t * LANES % half, t * LANES % half + LANES)
            ours = jnp.logical_xor(swap, t * LANES >= half)
            tiles[t] = jnp.where(ours, other[:, lane], mine[:, lane]) * (1.0 / points)
        ph = (turn_re[...], turn_im[...])
        back = (ph[0], -ph[1])
        row = lax.broadcasted_iota(jnp.int32, ph[0].shape, 0)
        g = []
        for e in range(blocks):
            down = [tiles[t, e * blocks : (e + 1) * blocks, :] for t in range(count)]
            across = [tiles[t, pl.ds(e, blocks, stride=blocks), :] for t in range(count)]
            down, across = jnp.concatenate(down, axis=1), jnp.concatenate(across, axis=1)
            re = jnp.where(row <= e, down, across)
            im = jnp.where(row < e, across, jnp.where(row > e, -down, 0.0))
            column = (ph[0][e : e + 1], ph[1][e : e + 1])
            g.append(cmul(cmul(back, (re, im)), column))
        ys = g[:MODES]
        for sweep in range(ITERS):
            done = []
            for v in ys:
                for q in done:
                    part = cmul(row_dot(q, v), q)
                    v = (v[0] - part[0], v[1] - part[1])
                length = jnp.sqrt(jnp.sum(v[0] * v[0] + v[1] * v[1], axis=0, keepdims=True))
                done.append((v[0] / length, v[1] / length))
            ys = []
            for q in done:
                re, im = jnp.zeros_like(q[0]), jnp.zeros_like(q[0])
                for e in range(blocks):
                    part = cmul(g[e], (q[0][e : e + 1], q[1][e : e + 1]))
                    re, im = re + part[0], im + part[1]
                ys.append((re, im))
        for m, (q, y) in enumerate(zip(done, ys)):
            level = row_dot(q, y)[0]
            levels[m : m + 1, :] = level
            factor = jnp.where(kept[...] > m, 1.0, 0.0) / jnp.sqrt(level)
            re, im = cmul(ph, q)
            re, im = re * factor, im * factor
            for t in range(count):
                lane = slice(t * LANES, (t + 1) * LANES)
                basis[t, 2 * m * blocks : (2 * m + 1) * blocks, :] = re[:, lane]
                basis[t, (2 * m + 1) * blocks : (2 * m + 2) * blocks, :] = im[:, lane]
        owned = energy.shape[1]
        bins = levels.shape[1]
        turned = pltpu.roll(levels[...], (bins - core[1] * owned) % bins, 1)
        energy[...] = turned[:MODES, :owned]

    where = []
    for re, im in spectra_refs:
        where += [(re, im, n * LANES) for n in range(re.shape[0] // LANES)]
    for m in range(MODES):
        total_re, total_im = None, None
        for b, (re, im, base) in enumerate(where):
            u = (re[base : base + LANES, :], im[base : base + LANES, :])
            q = [basis[step, pl.ds((2 * m + n) * blocks + b, 1), :] for n in (0, 1)]
            part = cmul(u, q)
            total_re = part[0] if b == 0 else total_re + part[0]
            total_im = part[1] if b == 0 else total_im + part[1]
        modes[m, 0] = total_re
        modes[m, 1] = total_im


def finish(blocks, points, owned, core, mine, other, turn, kept, parts):
    square, half = mine.shape
    bins = 2 * half
    flat = [a for part in parts for a in part]
    whole = lambda a: pl.BlockSpec(a.shape, lambda i, c: (0, 0))
    kept = kept.reshape(1, bins)
    small = [mine, other, *turn, kept]
    return pl.pallas_call(
        lambda *refs: finish_kernel(blocks, points, len(parts), *refs),
        grid_spec=pltpu.PrefetchScalarGridSpec(
            num_scalar_prefetch=1,
            grid=(bins // LANES,),
            in_specs=[whole(a) for a in small]
            + [pl.BlockSpec((a.shape[0], LANES), lambda i, c: (0, i)) for a in flat],
            out_specs=[
                pl.BlockSpec((MODES, owned), lambda i, c: (0, 0)),
                pl.BlockSpec((MODES, 2, LANES, LANES), lambda i, c: (0, 0, 0, i)),
            ],
            scratch_shapes=[
                pltpu.VMEM((bins // LANES, square, LANES), jnp.float32),
                pltpu.VMEM((bins // LANES, 2 * MODES * blocks, LANES), jnp.float32),
                pltpu.VMEM((8, bins), jnp.float32),
            ],
        ),
        out_shape=[
            jax.ShapeDtypeStruct((MODES, owned), jnp.float32),
            jax.ShapeDtypeStruct((MODES, 2, LANES, bins), jnp.float32),
        ],
        compiler_params=SMALL,
        cost_estimate=pl.CostEstimate(
            flops=16 * MODES * blocks * LANES * bins, bytes_accessed=6 * 2**20, transcendentals=0
        ),
    )(core, *small, *in_hbm(flat))


def gram_of(u, blocks):
    pairs = []
    for b, e in pair_list(blocks):
        pairs.append(jnp.sum(u[0][b] * u[0][e] + u[1][b] * u[1][e], axis=0))
        if e > b:
            pairs.append(jnp.sum(u[0][b] * u[1][e] - u[1][b] * u[0][e], axis=0))
    return jnp.stack(pairs, axis=0)


def plain(signal, offsets, pairing, modes_kept):
    rows, blocks, points = signal.shape
    ranks = lax.axis_size("freq")
    rank = lax.axis_index("freq")
    frames = rows * ranks
    bins = frames // 2
    own = points // ranks
    order = pairing.reshape(ranks, own // 2, 2).transpose(0, 2, 1).reshape(-1)
    packed = jnp.take(signal, order, axis=2).reshape(rows, blocks, ranks, own)
    packed = packed.transpose(2, 0, 1, 3)
    series = lax.all_to_all(packed, "freq", split_axis=0, concat_axis=0, tiled=True)
    series = series.reshape(frames, blocks * own)
    table = jnp.asarray(transform_table(frames))
    spectra = lax.dot_general(series, table, (((0,), (0,)), ((), ())), precision=precise)
    spectra = spectra.reshape(blocks, own, 2, bins)
    u = (spectra[:, :, 0], spectra[:, :, 1])
    sums = sum_over(gram_of(u, blocks), "freq") * (1.0 / points)
    g_re = [[None] * blocks for _ in range(blocks)]
    g_im = [[None] * blocks for _ in range(blocks)]
    at = 0
    for b in range(blocks):
        for e in range(b, blocks):
            g_re[b][e] = g_re[e][b] = sums[at]
            at += 1
            if e > b:
                g_im[b][e], g_im[e][b] = sums[at], -sums[at]
                at += 1
            else:
                g_im[b][b] = jnp.zeros_like(sums[0])
    g = (
        jnp.stack([jnp.stack(row) for row in g_re]),
        jnp.stack([jnp.stack(row) for row in g_im]),
    )
    turn = phase_table(offsets, bins, frames)
    both = cmul((turn[0][:, None], -turn[1][:, None]), (turn[0][None], turn[1][None]))
    basis, energy = leading_basis(cmul(both, g))
    live = jnp.arange(MODES, dtype=jnp.int32)[:, None] < modes_kept[None, :]
    factor = live.astype(jnp.float32) / jnp.sqrt(energy)
    modes = []
    for m in range(MODES):
        q = cmul(turn, basis[m])
        q = (q[0] * factor[m], q[1] * factor[m])
        re = jnp.sum(u[0] * q[0][:, None] - u[1] * q[1][:, None], axis=0)
        im = jnp.sum(u[0] * q[1][:, None] + u[1] * q[0][:, None], axis=0)
        modes.append(jnp.stack([re, im]))
    held = lax.dynamic_slice_in_dim(energy, rank * (bins // ranks), bins // ranks, axis=1)
    return held, jnp.stack(modes)


CHUNKS = (2, 6)


def swap_with(values, step):
    ranks = lax.axis_size("freq")
    return lax.ppermute(values, "freq", [(i, i ^ step) for i in range(ranks)])


def tiled(signal, offsets, pairing, modes_kept):
    rows, blocks, points = signal.shape
    ranks = lax.axis_size("freq")
    rank = lax.axis_index("freq")
    bins = rows * ranks // 2
    core = (rank & 1).reshape(1)
    turn = phase_table(offsets, bins, rows * ranks)
    tables = [jnp.asarray(t) for t in split_table(rows * ranks)]
    got, first = [], 0
    for count in CHUNKS:
        part = pack(signal, pairing, first, count)
        signal, part = lax.optimization_barrier((signal, part))
        got.append(lax.all_to_all(part, "freq", split_axis=0, concat_axis=0, tiled=True))
        first += count
    parts, gram = [], None
    for n, x in enumerate(got):
        final = n == len(got) - 1
        re, im, *grams = spectra(blocks, x.reshape(rows * ranks, -1), tables, core, parts, gram, final)
        parts.append((re, im))
        gram = grams[0]
    mine = gram + swap_with(grams[1], 1)
    step = 2
    while step < ranks:
        mine = mine + swap_with(mine, step)
        step *= 2
    other = swap_with(mine, 1)
    energy, modes = finish(
        blocks, points, bins // ranks, jnp.stack([rank & 1, rank]), mine, other, turn, modes_kept, parts
    )
    return energy, modes


def local(signal, offsets, pairing, modes_kept):
    rows, blocks, points = signal.shape
    ranks = lax.axis_size("freq")
    bins = rows * ranks // 2
    fits = points == ranks * LANES and rows % 16 == 0 and ranks >= GROUP and ranks & (ranks - 1) == 0
    fits = fits and bins % (2 * LANES) == 0 and blocks == sum(CHUNKS) == 8
    energy, modes = (tiled if fits else plain)(signal, offsets, pairing, modes_kept)
    modes = modes.reshape(MODES, 2, 2, points // ranks // 2, bins)
    return energy.T, modes.transpose(4, 0, 1, 2, 3)


def solution(mesh):
    placed = (P("freq", None, "groups"), P(), P("groups"), P())
    return jax.shard_map(
        local,
        mesh=mesh,
        in_specs=placed,
        out_specs=(P("freq", "groups"), P(None, None, None, None, ("groups", "freq"))),
        check_vma=False,
    )
```

```python
import math

import jax
import jax.numpy as jnp
import ml_dtypes
import numpy as np
from jax import lax
from jax.experimental import pallas as pl
from jax.experimental.pallas import tpu as pltpu
from jax.sharding import PartitionSpec as P

MODES = 4
ITERS = 3
precise = lax.Precision.HIGHEST


def transform_table(frames):
    steps = np.arange(frames)
    shape = 0.5 - 0.5 * np.cos(2.0 * np.pi * steps / frames)
    window = shape / np.sqrt(np.sum(shape * shape))
    phase = (steps[:, None] * np.arange(frames // 2)[None, :] % frames) * (2.0 * np.pi / frames)
    table = np.concatenate([np.cos(phase), -np.sin(phase)], axis=1) * window[:, None]
    return table.astype(np.float32)


def phase_table(offsets, bins, frames):
    steps = jnp.arange(bins, dtype=jnp.int32)[None, :] * offsets[:, None] % frames
    angle = steps.astype(jnp.float32) * (2.0 * math.pi / frames)
    return jnp.cos(angle), -jnp.sin(angle)


def sum_over(values, axis):
    size = lax.axis_size(axis)
    if size & (size - 1):
        return lax.psum(values, axis)
    step = 1
    while step < size:
        values = values + lax.ppermute(values, axis, [(i, i ^ step) for i in range(size)])
        step *= 2
    return values


def cmul(a, b):
    return a[0] * b[0] - a[1] * b[1], a[0] * b[1] + a[1] * b[0]


def cdot(a, b):
    return (
        jnp.sum(a[0] * b[0] + a[1] * b[1], axis=0, keepdims=True),
        jnp.sum(a[0] * b[1] - a[1] * b[0], axis=0, keepdims=True),
    )


def times_gram(g, v):
    re = jnp.sum(g[0] * v[0][None] - g[1] * v[1][None], axis=1)
    im = jnp.sum(g[0] * v[1][None] + g[1] * v[0][None], axis=1)
    return re, im


def leading_basis(g):
    blocks, bins = g[0].shape[0], g[0].shape[-1]
    ys = [(g[0][:, m], g[1][:, m]) for m in range(MODES)]
    for sweep in range(ITERS):
        done = []
        for v in ys:
            for q in done:
                part = cmul(cdot(q, v), q)
                v = (v[0] - part[0], v[1] - part[1])
            length = jnp.sqrt(jnp.sum(v[0] * v[0] + v[1] * v[1], axis=0, keepdims=True))
            done.append((v[0] / length, v[1] / length))
        ys = [times_gram(g, q) for q in done]
    energy = jnp.concatenate([cdot(q, y)[0] for q, y in zip(done, ys)], axis=0)
    return done, energy


LANES = 128
GROUP = 4
VMEM = pltpu.CompilerParams(vmem_limit_bytes=60 * 2**20)
SMALL = pltpu.CompilerParams(vmem_limit_bytes=50 * 2**20)


def split_table(frames):
    table = transform_table(frames).reshape(frames, 2, -1, LANES)
    table = table.transpose(0, 2, 1, 3).reshape(frames, frames)
    high = table.astype(ml_dtypes.bfloat16)
    low = (table - high.astype(np.float32)).astype(ml_dtypes.bfloat16)
    return high, low


def two_terms(x):
    high = x.astype(jnp.bfloat16)
    return high, (x - high.astype(jnp.float32)).astype(jnp.bfloat16)


def three_terms(x):
    high, rest = x.astype(jnp.bfloat16), None
    rest = x - high.astype(jnp.float32)
    mid = rest.astype(jnp.bfloat16)
    return high, mid, (rest - mid.astype(jnp.float32)).astype(jnp.bfloat16)


def dot(a, b):
    return jnp.dot(a, b, preferred_element_type=jnp.float32)


def in_hbm(arrays):
    return [pltpu.with_memory_space_constraint(a, pltpu.HBM) for a in arrays]


def pack_kernel(blocks, first, count, strips, *refs):
    signals, pairing, out, one_row, low_pick, total = refs[:strips], *refs[strips:]
    step = pl.program_id(0)
    rows = signals[0].shape[0] // blocks
    ranks = out.shape[0]
    depth = strips * LANES

    @pl.when(step == 0)
    def _():
        place = lax.broadcasted_iota(jnp.int32, (LANES, LANES), 1)
        source = lax.broadcasted_iota(jnp.int32, (LANES, LANES), 0)
        half = LANES // 2
        wanted = jnp.where(place < half, 2 * place, 2 * (place - half) + 1)
        turn = (wanted == source).astype(jnp.float32).astype(jnp.bfloat16)
        lines = pairing[...]
        upper = (lines >> 5).astype(jnp.float32).astype(jnp.bfloat16)
        lower = (lines & 31).astype(jnp.float32).astype(jnp.bfloat16)
        one_row[...] = (dot(upper, turn) * 32.0 + dot(lower, turn)).astype(jnp.int32)
        total[...] = jnp.zeros_like(total)
        for n in range(ranks):
            low_pick[:, n * LANES : (n + 1) * LANES] = jnp.where(
                source == one_row[n : n + 1, :] % LANES, 1.0, 0.0
            ).astype(jnp.bfloat16)

    x = jnp.concatenate(
        [
            jnp.concatenate([strip[pl.ds(b, rows, stride=blocks), :] for strip in signals], axis=1)
            for b in range(first, first + count)
        ],
        axis=0,
    )
    stacked = jnp.concatenate(three_terms(x), axis=0)
    third = stacked.shape[0] // 3
    here = [
        jnp.where(one_row[...] // LANES == step * strips + n, 1.0, 0.0) for n in range(strips)
    ]
    for at in range(0, ranks, GROUP):
        pick = []
        for n in range(at, at + GROUP):
            spot = low_pick[:, n * LANES : (n + 1) * LANES]
            strip = [
                spot * jnp.broadcast_to(line[n : n + 1], spot.shape).astype(jnp.bfloat16) for line in here
            ]
            pick.append(jnp.concatenate(strip, axis=0))
        got = dot(stacked, jnp.concatenate(pick, axis=1))
        spot = (slice(None), slice(at * LANES, (at + GROUP) * LANES))
        total[spot] += got[:third] + got[third : 2 * third] + got[2 * third :]

    @pl.when(step == pl.num_programs(0) - 1)
    def _():
        for n in range(ranks):
            for b in range(count):
                out[n, :, b * LANES : (b + 1) * LANES] = total[
                    b * rows : (b + 1) * rows, n * LANES : (n + 1) * LANES
                ]


def pack(signal, pairing, first, count):
    rows, blocks, points = signal.shape
    strips = 4
    ranks = points // LANES
    shape = (ranks, rows, count * LANES)
    return pl.pallas_call(
        lambda *refs: pack_kernel(blocks, first, count, strips, *refs),
        grid=(points // (strips * LANES),),
        in_specs=[
            pl.BlockSpec((rows * blocks, LANES), lambda i, n=n: (0, strips * i + n))
            for n in range(strips)
        ]
        + [pl.BlockSpec((ranks, LANES), lambda i: (0, 0))],
        out_specs=pl.BlockSpec(shape, lambda i: (0, 0, 0)),
        scratch_shapes=[
            pltpu.VMEM((ranks, LANES), jnp.int32),
            pltpu.VMEM((LANES, points), jnp.bfloat16),
            pltpu.VMEM((rows * count, points), jnp.float32),
        ],
        out_shape=jax.ShapeDtypeStruct(shape, jnp.float32),
        compiler_params=VMEM,
        cost_estimate=pl.CostEstimate(
            flops=6 * rows * count * points * points, bytes_accessed=8 * 2**20, transcendentals=0
        ),
    )(*[signal.reshape(rows * blocks, points)] * strips, pairing.reshape(-1, LANES))


def pair_list(blocks):
    return [(b, e) for b in range(blocks) for e in range(b, blocks)]


def gram_tile(parts, blocks, gram):
    where = []
    for re, im in parts:
        where += [(re, im, n * LANES) for n in range(re.shape[0] // LANES)]
    fresh = len(where)
    start = fresh - parts[-1][0].shape[0] // LANES
    todo = [(b, e) for e in range(start, fresh) for b in range(e + 1)]
    most = 14
    for first in range(0, len(todo), most):
        chunk = todo[first : first + most]
        used = sorted({b for b, _ in chunk} | {e for _, e in chunk})

        def body(i, sums):
            spot = pl.multiple_of(i * 8, 8)
            u = {}
            for b in used:
                re, im, base = where[b]
                u[b] = (re[pl.ds(base + spot, 8), :], im[pl.ds(base + spot, 8), :])
            out = []
            for b, e in chunk:
                (br, bi), (er, ei) = u[b], u[e]
                out.append(br * er + bi * ei)
                if b != e:
                    out.append(br * ei - bi * er)
            return tuple(s + o for s, o in zip(sums, out))

        rows = []
        for b, e in chunk:
            rows += [e * blocks + b] if b == e else [e * blocks + b, b * blocks + e]
        zero = jnp.zeros((8, gram.shape[1]), jnp.float32)
        sums = lax.fori_loop(0, LANES // 8, body, (zero,) * len(rows), unroll=True)
        for row, value in zip(rows, sums):
            gram[row : row + 1, :] = jnp.sum(value, axis=0, keepdims=True)


def spectra_kernel(blocks, others, final, core, x, high, low, *refs):
    parts = [(refs[2 * n], refs[2 * n + 1]) for n in range(others)]
    refs = refs[2 * others :]
    before, refs = (refs[0], refs[1:]) if others else (None, refs)
    (re, im), grams, (x_high, x_low, gram) = refs[:2], refs[2:-3], refs[-3:]
    step = pl.program_id(0)

    def put(got):
        re[...] = got[:, :LANES]
        im[...] = got[:, LANES:]

    @pl.when(step == 0)
    def _():
        depth = 2 * LANES
        got = None
        for at in range(0, x.shape[0], depth):
            spot = (slice(None), slice(at, at + depth))
            x_high[spot], x_low[spot] = terms = two_terms(x[at : at + depth, :].T)
            w = (high[at : at + depth, :], low[at : at + depth, :])
            part = dot(terms[0], w[0]) + dot(terms[1], w[0]) + dot(terms[0], w[1])
            got = part if at == 0 else got + part
        put(got)

    @pl.when(step > 0)
    def _():
        put(dot(x_high[...], high[...]) + dot(x_low[...], high[...]) + dot(x_high[...], low[...]))

    gram[...] = before[...] if others else jnp.zeros_like(gram)
    gram_tile(parts + [(re, im)], blocks, gram)
    if final:
        half = step // (pl.num_programs(0) // 2)
        lane = pl.multiple_of(step % (pl.num_programs(0) // 2) * LANES, LANES)

        @pl.when(half == core[0])
        def _():
            grams[0][:, pl.ds(lane, LANES)] = gram[...]

        @pl.when(half != core[0])
        def _():
            grams[1][:, pl.ds(lane, LANES)] = gram[...]
    else:
        grams[0][...] = gram[...]


def spectra(blocks, x, tables, core, others=(), before=None, final=False):
    frames, width = x.shape
    bins = frames // 2
    held = pl.BlockSpec((width, LANES), lambda i, c: (0, i))
    shape = pltpu.HBM((width, bins), jnp.float32)
    flat = [a for part in others for a in part] + ([before] if others else [])
    in_specs = [pl.BlockSpec(memory_space=pltpu.VMEM)]
    in_specs += [pl.BlockSpec((frames, 2 * LANES), lambda i, c: (0, i))] * 2
    in_specs += [pl.BlockSpec((a.shape[0], LANES), lambda i, c: (0, i)) for a in flat]
    square = blocks * blocks
    if final:
        out_specs = [held] * 2 + [pl.BlockSpec((square, bins // 2), lambda i, c: (0, 0))] * 2
        out_shape = [shape] * 2 + [jax.ShapeDtypeStruct((square, bins // 2), jnp.float32)] * 2
    else:
        out_specs = [held] * 2 + [pl.BlockSpec((square, LANES), lambda i, c: (0, i))]
        out_shape = [shape] * 2 + [jax.ShapeDtypeStruct((square, bins), jnp.float32)]
    return pl.pallas_call(
        lambda *refs: spectra_kernel(blocks, len(others), final, *refs),
        grid_spec=pltpu.PrefetchScalarGridSpec(
            num_scalar_prefetch=1,
            grid=(bins // LANES,),
            in_specs=in_specs,
            out_specs=out_specs,
            scratch_shapes=[pltpu.VMEM((width, frames), jnp.bfloat16)] * 2
            + [pltpu.VMEM((square, LANES), jnp.float32)],
        ),
        out_shape=out_shape,
        compiler_params=SMALL,
        cost_estimate=pl.CostEstimate(
            flops=6 * width * frames * frames, bytes_accessed=12 * 2**20, transcendentals=0
        ),
    )(core, x, *in_hbm([*tables, *flat]))


def row_dot(a, b):
    return (
        jnp.sum(a[0] * b[0] + a[1] * b[1], axis=0, keepdims=True),
        jnp.sum(a[0] * b[1] - a[1] * b[0], axis=0, keepdims=True),
    )


def finish_kernel(blocks, points, parts, core, mine, other, turn_re, turn_im, kept, *refs):
    sources, refs = refs[: 2 * parts], refs[2 * parts :]
    energy, modes, tiles, basis, levels, made, come, gone = refs[:8]
    held = refs[8:]
    steps = come.shape[0]

    def arrivals(t):
        lane = slice(t * LANES, (t + 1) * LANES)
        return [
            pltpu.make_async_copy(source.at[:, lane], place.at[t], come.at[t, n])
            for n, (source, place) in enumerate(zip(sources, held))
        ]

    def departure(t):
        lane = slice(t * LANES, (t + 1) * LANES)
        return pltpu.make_async_copy(made.at[t], modes.at[:, :, :, lane], gone.at[t])

    for t in range(steps):
        for copy in arrivals(t):
            copy.start()

    def make_basis():
        swap = core[0] == 1
        half = mine.shape[1]
        count = 2 * half // LANES
        for t in range(count):
            lane = slice(t * LANES % half, t * LANES % half + LANES)
            ours = jnp.logical_xor(swap, t * LANES >= half)
            tiles[t] = jnp.where(ours, other[:, lane], mine[:, lane]) * (1.0 / points)
        ph = (turn_re[...], turn_im[...])
        back = (ph[0], -ph[1])
        row = lax.broadcasted_iota(jnp.int32, ph[0].shape, 0)
        g = []
        for e in range(blocks):
            down = [tiles[t, e * blocks : (e + 1) * blocks, :] for t in range(count)]
            across = [tiles[t, pl.ds(e, blocks, stride=blocks), :] for t in range(count)]
            down, across = jnp.concatenate(down, axis=1), jnp.concatenate(across, axis=1)
            re = jnp.where(row <= e, down, across)
            im = jnp.where(row < e, across, jnp.where(row > e, -down, 0.0))
            column = (ph[0][e : e + 1], ph[1][e : e + 1])
            g.append(cmul(cmul(back, (re, im)), column))
        ys = g[:MODES]
        for sweep in range(ITERS):
            done = []
            for v in ys:
                for q in done:
                    part = cmul(row_dot(q, v), q)
                    v = (v[0] - part[0], v[1] - part[1])
                length = jnp.sqrt(jnp.sum(v[0] * v[0] + v[1] * v[1], axis=0, keepdims=True))
                done.append((v[0] / length, v[1] / length))
            ys = []
            for q in done:
                re, im = jnp.zeros_like(q[0]), jnp.zeros_like(q[0])
                for e in range(blocks):
                    part = cmul(g[e], (q[0][e : e + 1], q[1][e : e + 1]))
                    re, im = re + part[0], im + part[1]
                ys.append((re, im))
        for m, (q, y) in enumerate(zip(done, ys)):
            level = row_dot(q, y)[0]
            levels[m : m + 1, :] = level
            factor = jnp.where(kept[...] > m, 1.0, 0.0) / jnp.sqrt(level)
            re, im = cmul(ph, q)
            re, im = re * factor, im * factor
            for t in range(count):
                lane = slice(t * LANES, (t + 1) * LANES)
                basis[t, 2 * m * blocks : (2 * m + 1) * blocks, :] = re[:, lane]
                basis[t, (2 * m + 1) * blocks : (2 * m + 2) * blocks, :] = im[:, lane]
        owned = energy.shape[1]
        bins = levels.shape[1]
        turned = pltpu.roll(levels[...], (bins - core[1] * owned) % bins, 1)
        energy[...] = turned[:MODES, :owned]

    make_basis()
    for t in range(steps):
        for copy in arrivals(t):
            copy.wait()
        where = []
        for n in range(parts):
            re, im = held[2 * n].at[t], held[2 * n + 1].at[t]
            where += [(re, im, n * LANES) for n in range(re.shape[0] // LANES)]
        for m in range(MODES):
            total = None
            for b, (re, im, base) in enumerate(where):
                u = (re[base : base + LANES, :], im[base : base + LANES, :])
                q = [basis[t, (2 * m + n) * blocks + b : (2 * m + n) * blocks + b + 1, :] for n in (0, 1)]
                part = cmul(u, q)
                total = part if b == 0 else (total[0] + part[0], total[1] + part[1])
            made[t, m, 0] = total[0]
            made[t, m, 1] = total[1]
        departure(t).start()
    for t in range(steps):
        departure(t).wait()


def finish(blocks, points, owned, core, mine, other, turn, kept, parts):
    square, half = mine.shape
    bins = 2 * half
    flat = [a for part in parts for a in part]
    kept = kept.reshape(1, bins)
    small = [mine, other, *turn, kept]
    steps = bins // LANES
    vmem = pl.BlockSpec(memory_space=pltpu.VMEM)
    return pl.pallas_call(
        lambda *refs: finish_kernel(blocks, points, len(parts), *refs),
        grid_spec=pltpu.PrefetchScalarGridSpec(
            num_scalar_prefetch=1,
            grid=(1,),
            in_specs=[vmem] * len(small) + [pl.BlockSpec(memory_space=pltpu.HBM)] * len(flat),
            out_specs=[vmem, pl.BlockSpec(memory_space=pltpu.HBM)],
            scratch_shapes=[
                pltpu.VMEM((steps, square, LANES), jnp.float32),
                pltpu.VMEM((steps, 2 * MODES * blocks, LANES), jnp.float32),
                pltpu.VMEM((8, bins), jnp.float32),
                pltpu.VMEM((steps, MODES, 2, LANES, LANES), jnp.float32),
                pltpu.SemaphoreType.DMA((steps, len(flat))),
                pltpu.SemaphoreType.DMA((steps,)),
            ]
            + [pltpu.VMEM((steps, a.shape[0], LANES), jnp.float32) for a in flat],
        ),
        out_shape=[
            jax.ShapeDtypeStruct((MODES, owned), jnp.float32),
            jax.ShapeDtypeStruct((MODES, 2, LANES, bins), jnp.float32),
        ],
        compiler_params=SMALL,
        cost_estimate=pl.CostEstimate(
            flops=16 * MODES * blocks * LANES * bins, bytes_accessed=6 * 2**20, transcendentals=0
        ),
    )(core, *small, *in_hbm(flat))


def gram_of(u, blocks):
    pairs = []
    for b, e in pair_list(blocks):
        pairs.append(jnp.sum(u[0][b] * u[0][e] + u[1][b] * u[1][e], axis=0))
        if e > b:
            pairs.append(jnp.sum(u[0][b] * u[1][e] - u[1][b] * u[0][e], axis=0))
    return jnp.stack(pairs, axis=0)


def plain(signal, offsets, pairing, modes_kept):
    rows, blocks, points = signal.shape
    ranks = lax.axis_size("freq")
    rank = lax.axis_index("freq")
    frames = rows * ranks
    bins = frames // 2
    own = points // ranks
    order = pairing.reshape(ranks, own // 2, 2).transpose(0, 2, 1).reshape(-1)
    packed = jnp.take(signal, order, axis=2).reshape(rows, blocks, ranks, own)
    packed = packed.transpose(2, 0, 1, 3)
    series = lax.all_to_all(packed, "freq", split_axis=0, concat_axis=0, tiled=True)
    series = series.reshape(frames, blocks * own)
    table = jnp.asarray(transform_table(frames))
    spectra = lax.dot_general(series, table, (((0,), (0,)), ((), ())), precision=precise)
    spectra = spectra.reshape(blocks, own, 2, bins)
    u = (spectra[:, :, 0], spectra[:, :, 1])
    sums = sum_over(gram_of(u, blocks), "freq") * (1.0 / points)
    g_re = [[None] * blocks for _ in range(blocks)]
    g_im = [[None] * blocks for _ in range(blocks)]
    at = 0
    for b in range(blocks):
        for e in range(b, blocks):
            g_re[b][e] = g_re[e][b] = sums[at]
            at += 1
            if e > b:
                g_im[b][e], g_im[e][b] = sums[at], -sums[at]
                at += 1
            else:
                g_im[b][b] = jnp.zeros_like(sums[0])
    g = (
        jnp.stack([jnp.stack(row) for row in g_re]),
        jnp.stack([jnp.stack(row) for row in g_im]),
    )
    turn = phase_table(offsets, bins, frames)
    both = cmul((turn[0][:, None], -turn[1][:, None]), (turn[0][None], turn[1][None]))
    basis, energy = leading_basis(cmul(both, g))
    live = jnp.arange(MODES, dtype=jnp.int32)[:, None] < modes_kept[None, :]
    factor = live.astype(jnp.float32) / jnp.sqrt(energy)
    modes = []
    for m in range(MODES):
        q = cmul(turn, basis[m])
        q = (q[0] * factor[m], q[1] * factor[m])
        re = jnp.sum(u[0] * q[0][:, None] - u[1] * q[1][:, None], axis=0)
        im = jnp.sum(u[0] * q[1][:, None] + u[1] * q[0][:, None], axis=0)
        modes.append(jnp.stack([re, im]))
    held = lax.dynamic_slice_in_dim(energy, rank * (bins // ranks), bins // ranks, axis=1)
    return held, jnp.stack(modes)


CHUNKS = (2, 6)


def swap_with(values, step):
    ranks = lax.axis_size("freq")
    return lax.ppermute(values, "freq", [(i, i ^ step) for i in range(ranks)])


def tiled(signal, offsets, pairing, modes_kept):
    rows, blocks, points = signal.shape
    ranks = lax.axis_size("freq")
    rank = lax.axis_index("freq")
    bins = rows * ranks // 2
    core = (rank & 1).reshape(1)
    turn = phase_table(offsets, bins, rows * ranks)
    tables = [jnp.asarray(t) for t in split_table(rows * ranks)]
    got, first = [], 0
    for count in CHUNKS:
        part = pack(signal, pairing, first, count)
        signal, part = lax.optimization_barrier((signal, part))
        got.append(lax.all_to_all(part, "freq", split_axis=0, concat_axis=0, tiled=True))
        first += count
    parts, gram = [], None
    for n, x in enumerate(got):
        final = n == len(got) - 1
        re, im, *grams = spectra(blocks, x.reshape(rows * ranks, -1), tables, core, parts, gram, final)
        parts.append((re, im))
        gram = grams[0]
    mine = gram + swap_with(grams[1], 1)
    step = 2
    while step < ranks:
        mine = mine + swap_with(mine, step)
        step *= 2
    other = swap_with(mine, 1)
    energy, modes = finish(
        blocks, points, bins // ranks, jnp.stack([rank & 1, rank]), mine, other, turn, modes_kept, parts
    )
    return energy, modes


def local(signal, offsets, pairing, modes_kept):
    rows, blocks, points = signal.shape
    ranks = lax.axis_size("freq")
    bins = rows * ranks // 2
    fits = points == ranks * LANES and rows % 16 == 0 and ranks >= GROUP and ranks & (ranks - 1) == 0
    fits = fits and bins % (2 * LANES) == 0 and blocks == sum(CHUNKS) == 8
    energy, modes = (tiled if fits else plain)(signal, offsets, pairing, modes_kept)
    modes = modes.reshape(MODES, 2, 2, points // ranks // 2, bins)
    return energy.T, modes.transpose(4, 0, 1, 2, 3)


def solution(mesh):
    placed = (P("freq", None, "groups"), P(), P("groups"), P())
    return jax.shard_map(
        local,
        mesh=mesh,
        in_specs=placed,
        out_specs=(P("freq", "groups"), P(None, None, None, None, ("groups", "freq"))),
        check_vma=False,
    )
```

```python
import math

import jax
import jax.numpy as jnp
import ml_dtypes
import numpy as np
from jax import lax
from jax.experimental import pallas as pl
from jax.experimental.pallas import tpu as pltpu
from jax.sharding import PartitionSpec as P

MODES = 4
ITERS = 3
precise = lax.Precision.HIGHEST


def transform_table(frames):
    steps = np.arange(frames)
    shape = 0.5 - 0.5 * np.cos(2.0 * np.pi * steps / frames)
    window = shape / np.sqrt(np.sum(shape * shape))
    phase = (steps[:, None] * np.arange(frames // 2)[None, :] % frames) * (2.0 * np.pi / frames)
    table = np.concatenate([np.cos(phase), -np.sin(phase)], axis=1) * window[:, None]
    return table.astype(np.float32)


def phase_table(offsets, bins, frames):
    steps = jnp.arange(bins, dtype=jnp.int32)[None, :] * offsets[:, None] % frames
    angle = steps.astype(jnp.float32) * (2.0 * math.pi / frames)
    return jnp.cos(angle), -jnp.sin(angle)


def sum_over(values, axis):
    size = lax.axis_size(axis)
    if size & (size - 1):
        return lax.psum(values, axis)
    step = 1
    while step < size:
        values = values + lax.ppermute(values, axis, [(i, i ^ step) for i in range(size)])
        step *= 2
    return values


def cmul(a, b):
    return a[0] * b[0] - a[1] * b[1], a[0] * b[1] + a[1] * b[0]


def cdot(a, b):
    return (
        jnp.sum(a[0] * b[0] + a[1] * b[1], axis=0, keepdims=True),
        jnp.sum(a[0] * b[1] - a[1] * b[0], axis=0, keepdims=True),
    )


def times_gram(g, v):
    re = jnp.sum(g[0] * v[0][None] - g[1] * v[1][None], axis=1)
    im = jnp.sum(g[0] * v[1][None] + g[1] * v[0][None], axis=1)
    return re, im


def leading_basis(g):
    blocks, bins = g[0].shape[0], g[0].shape[-1]
    ys = [(g[0][:, m], g[1][:, m]) for m in range(MODES)]
    for sweep in range(ITERS):
        done = []
        for v in ys:
            for q in done:
                part = cmul(cdot(q, v), q)
                v = (v[0] - part[0], v[1] - part[1])
            length = jnp.sqrt(jnp.sum(v[0] * v[0] + v[1] * v[1], axis=0, keepdims=True))
            done.append((v[0] / length, v[1] / length))
        ys = [times_gram(g, q) for q in done]
    energy = jnp.concatenate([cdot(q, y)[0] for q, y in zip(done, ys)], axis=0)
    return done, energy


LANES = 128
GROUP = 4
VMEM = pltpu.CompilerParams(vmem_limit_bytes=60 * 2**20)
SMALL = pltpu.CompilerParams(vmem_limit_bytes=50 * 2**20)


def split_table(frames):
    table = transform_table(frames).reshape(frames, 2, -1, LANES)
    table = table.transpose(0, 2, 1, 3).reshape(frames, frames)
    high = table.astype(ml_dtypes.bfloat16)
    low = (table - high.astype(np.float32)).astype(ml_dtypes.bfloat16)
    return high, low


def two_terms(x):
    high = x.astype(jnp.bfloat16)
    return high, (x - high.astype(jnp.float32)).astype(jnp.bfloat16)


def three_terms(x):
    high, rest = x.astype(jnp.bfloat16), None
    rest = x - high.astype(jnp.float32)
    mid = rest.astype(jnp.bfloat16)
    return high, mid, (rest - mid.astype(jnp.float32)).astype(jnp.bfloat16)


def dot(a, b):
    return jnp.dot(a, b, preferred_element_type=jnp.float32)


def in_hbm(arrays):
    return [pltpu.with_memory_space_constraint(a, pltpu.HBM) for a in arrays]


def pack_kernel(blocks, first, count, strips, *refs):
    signals, pairing, out, one_row, low_pick, total = refs[:strips], *refs[strips:]
    step = pl.program_id(0)
    rows = signals[0].shape[0] // blocks
    ranks = out.shape[0]
    depth = strips * LANES

    @pl.when(step == 0)
    def _():
        place = lax.broadcasted_iota(jnp.int32, (LANES, LANES), 1)
        source = lax.broadcasted_iota(jnp.int32, (LANES, LANES), 0)
        half = LANES // 2
        wanted = jnp.where(place < half, 2 * place, 2 * (place - half) + 1)
        turn = (wanted == source).astype(jnp.float32).astype(jnp.bfloat16)
        lines = pairing[...]
        upper = (lines >> 5).astype(jnp.float32).astype(jnp.bfloat16)
        lower = (lines & 31).astype(jnp.float32).astype(jnp.bfloat16)
        one_row[...] = (dot(upper, turn) * 32.0 + dot(lower, turn)).astype(jnp.int32)
        total[...] = jnp.zeros_like(total)
        for n in range(ranks):
            low_pick[:, n * LANES : (n + 1) * LANES] = jnp.where(
                source == one_row[n : n + 1, :] % LANES, 1.0, 0.0
            ).astype(jnp.bfloat16)

    x = jnp.concatenate(
        [
            jnp.concatenate([strip[pl.ds(b, rows, stride=blocks), :] for strip in signals], axis=1)
            for b in range(first, first + count)
        ],
        axis=0,
    )
    stacked = jnp.concatenate(three_terms(x), axis=0)
    third = stacked.shape[0] // 3
    here = [
        jnp.where(one_row[...] // LANES == step * strips + n, 1.0, 0.0) for n in range(strips)
    ]
    for at in range(0, ranks, GROUP):
        pick = []
        for n in range(at, at + GROUP):
            spot = low_pick[:, n * LANES : (n + 1) * LANES]
            strip = [
                spot * jnp.broadcast_to(line[n : n + 1], spot.shape).astype(jnp.bfloat16) for line in here
            ]
            pick.append(jnp.concatenate(strip, axis=0))
        got = dot(stacked, jnp.concatenate(pick, axis=1))
        spot = (slice(None), slice(at * LANES, (at + GROUP) * LANES))
        total[spot] += got[:third] + got[third : 2 * third] + got[2 * third :]

    @pl.when(step == pl.num_programs(0) - 1)
    def _():
        for n in range(ranks):
            for b in range(count):
                out[n, :, b * LANES : (b + 1) * LANES] = total[
                    b * rows : (b + 1) * rows, n * LANES : (n + 1) * LANES
                ]


def pack(signal, pairing, first, count):
    rows, blocks, points = signal.shape
    strips = 8
    ranks = points // LANES
    shape = (ranks, rows, count * LANES)
    return pl.pallas_call(
        lambda *refs: pack_kernel(blocks, first, count, strips, *refs),
        grid=(points // (strips * LANES),),
        in_specs=[
            pl.BlockSpec((rows * blocks, LANES), lambda i, n=n: (0, strips * i + n))
            for n in range(strips)
        ]
        + [pl.BlockSpec((ranks, LANES), lambda i: (0, 0))],
        out_specs=pl.BlockSpec(shape, lambda i: (0, 0, 0)),
        scratch_shapes=[
            pltpu.VMEM((ranks, LANES), jnp.int32),
            pltpu.VMEM((LANES, points), jnp.bfloat16),
            pltpu.VMEM((rows * count, points), jnp.float32),
        ],
        out_shape=jax.ShapeDtypeStruct(shape, jnp.float32),
        compiler_params=VMEM,
        cost_estimate=pl.CostEstimate(
            flops=6 * rows * count * points * points, bytes_accessed=8 * 2**20, transcendentals=0
        ),
    )(*[signal.reshape(rows * blocks, points)] * strips, pairing.reshape(-1, LANES))


def pair_list(blocks):
    return [(b, e) for b in range(blocks) for e in range(b, blocks)]


def gram_tile(parts, blocks, gram):
    where = []
    for re, im in parts:
        where += [(re, im, n * LANES) for n in range(re.shape[0] // LANES)]
    fresh = len(where)
    start = fresh - parts[-1][0].shape[0] // LANES
    todo = [(b, e) for e in range(start, fresh) for b in range(e + 1)]
    most = 14
    for first in range(0, len(todo), most):
        chunk = todo[first : first + most]
        used = sorted({b for b, _ in chunk} | {e for _, e in chunk})

        def body(i, sums):
            spot = pl.multiple_of(i * 8, 8)
            u = {}
            for b in used:
                re, im, base = where[b]
                u[b] = (re[pl.ds(base + spot, 8), :], im[pl.ds(base + spot, 8), :])
            out = []
            for b, e in chunk:
                (br, bi), (er, ei) = u[b], u[e]
                out.append(br * er + bi * ei)
                if b != e:
                    out.append(br * ei - bi * er)
            return tuple(s + o for s, o in zip(sums, out))

        rows = []
        for b, e in chunk:
            rows += [e * blocks + b] if b == e else [e * blocks + b, b * blocks + e]
        zero = jnp.zeros((8, gram.shape[1]), jnp.float32)
        sums = lax.fori_loop(0, LANES // 8, body, (zero,) * len(rows), unroll=True)
        for row, value in zip(rows, sums):
            gram[row : row + 1, :] = jnp.sum(value, axis=0, keepdims=True)


def spectra_kernel(blocks, others, final, core, x, high, low, *refs):
    parts = [(refs[2 * n], refs[2 * n + 1]) for n in range(others)]
    refs = refs[2 * others :]
    before, refs = (refs[0], refs[1:]) if others else (None, refs)
    (re, im), grams, (x_high, x_low, gram) = refs[:2], refs[2:-3], refs[-3:]
    step = pl.program_id(0)

    def put(got):
        re[...] = got[:, :LANES]
        im[...] = got[:, LANES:]

    @pl.when(step == 0)
    def _():
        depth = 2 * LANES
        got = None
        for at in range(0, x.shape[0], depth):
            spot = (slice(None), slice(at, at + depth))
            x_high[spot], x_low[spot] = terms = two_terms(x[at : at + depth, :].T)
            w = (high[at : at + depth, :], low[at : at + depth, :])
            part = dot(terms[0], w[0]) + dot(terms[1], w[0]) + dot(terms[0], w[1])
            got = part if at == 0 else got + part
        put(got)

    @pl.when(step > 0)
    def _():
        put(dot(x_high[...], high[...]) + dot(x_low[...], high[...]) + dot(x_high[...], low[...]))

    gram[...] = before[...] if others else jnp.zeros_like(gram)
    gram_tile(parts + [(re, im)], blocks, gram)
    if final:
        half = step // (pl.num_programs(0) // 2)
        lane = pl.multiple_of(step % (pl.num_programs(0) // 2) * LANES, LANES)

        @pl.when(half == core[0])
        def _():
            grams[0][:, pl.ds(lane, LANES)] = gram[...]

        @pl.when(half != core[0])
        def _():
            grams[1][:, pl.ds(lane, LANES)] = gram[...]
    else:
        grams[0][...] = gram[...]


def spectra(blocks, x, tables, core, others=(), before=None, final=False):
    frames, width = x.shape
    bins = frames // 2
    held = pl.BlockSpec((width, LANES), lambda i, c: (0, i))
    shape = pltpu.HBM((width, bins), jnp.float32)
    flat = [a for part in others for a in part] + ([before] if others else [])
    in_specs = [pl.BlockSpec(memory_space=pltpu.VMEM)]
    in_specs += [pl.BlockSpec((frames, 2 * LANES), lambda i, c: (0, i))] * 2
    in_specs += [pl.BlockSpec((a.shape[0], LANES), lambda i, c: (0, i)) for a in flat]
    square = blocks * blocks
    if final:
        out_specs = [held] * 2 + [pl.BlockSpec((square, bins // 2), lambda i, c: (0, 0))] * 2
        out_shape = [shape] * 2 + [jax.ShapeDtypeStruct((square, bins // 2), jnp.float32)] * 2
    else:
        out_specs = [held] * 2 + [pl.BlockSpec((square, LANES), lambda i, c: (0, i))]
        out_shape = [shape] * 2 + [jax.ShapeDtypeStruct((square, bins), jnp.float32)]
    return pl.pallas_call(
        lambda *refs: spectra_kernel(blocks, len(others), final, *refs),
        grid_spec=pltpu.PrefetchScalarGridSpec(
            num_scalar_prefetch=1,
            grid=(bins // LANES,),
            in_specs=in_specs,
            out_specs=out_specs,
            scratch_shapes=[pltpu.VMEM((width, frames), jnp.bfloat16)] * 2
            + [pltpu.VMEM((square, LANES), jnp.float32)],
        ),
        out_shape=out_shape,
        compiler_params=SMALL,
        cost_estimate=pl.CostEstimate(
            flops=6 * width * frames * frames, bytes_accessed=12 * 2**20, transcendentals=0
        ),
    )(core, x, *in_hbm([*tables, *flat]))


def row_dot(a, b):
    return (
        jnp.sum(a[0] * b[0] + a[1] * b[1], axis=0, keepdims=True),
        jnp.sum(a[0] * b[1] - a[1] * b[0], axis=0, keepdims=True),
    )


def finish_kernel(blocks, points, parts, core, mine, other, turn_re, turn_im, kept, *refs):
    sources, refs = refs[: 2 * parts], refs[2 * parts :]
    energy, modes, tiles, basis, levels, made, come, gone = refs[:8]
    held = refs[8:]
    steps = come.shape[0]

    def arrivals(t):
        lane = pl.ds(pl.multiple_of(t * LANES, LANES), LANES)
        return [
            pltpu.make_async_copy(source.at[:, lane], place.at[t], come.at[t, n])
            for n, (source, place) in enumerate(zip(sources, held))
        ]

    def departure(t):
        lane = pl.ds(pl.multiple_of(t * LANES, LANES), LANES)
        return pltpu.make_async_copy(made.at[t], modes.at[:, :, :, lane], gone.at[t])

    for t in range(steps):
        for copy in arrivals(t):
            copy.start()

    def make_basis():
        swap = core[0] == 1
        half = mine.shape[1]
        count = 2 * half // LANES
        for t in range(count):
            lane = slice(t * LANES % half, t * LANES % half + LANES)
            ours = jnp.logical_xor(swap, t * LANES >= half)
            tiles[t] = jnp.where(ours, other[:, lane], mine[:, lane]) * (1.0 / points)
        ph = (turn_re[...], turn_im[...])
        back = (ph[0], -ph[1])
        row = lax.broadcasted_iota(jnp.int32, ph[0].shape, 0)
        g = []
        for e in range(blocks):
            down = [tiles[t, e * blocks : (e + 1) * blocks, :] for t in range(count)]
            across = [tiles[t, pl.ds(e, blocks, stride=blocks), :] for t in range(count)]
            down, across = jnp.concatenate(down, axis=1), jnp.concatenate(across, axis=1)
            re = jnp.where(row <= e, down, across)
            im = jnp.where(row < e, across, jnp.where(row > e, -down, 0.0))
            column = (ph[0][e : e + 1], ph[1][e : e + 1])
            g.append(cmul(cmul(back, (re, im)), column))
        ys = g[:MODES]
        for sweep in range(ITERS):
            done = []
            for v in ys:
                for q in done:
                    part = cmul(row_dot(q, v), q)
                    v = (v[0] - part[0], v[1] - part[1])
                length = jnp.sqrt(jnp.sum(v[0] * v[0] + v[1] * v[1], axis=0, keepdims=True))
                done.append((v[0] / length, v[1] / length))
            ys = []
            for q in done:
                re, im = jnp.zeros_like(q[0]), jnp.zeros_like(q[0])
                for e in range(blocks):
                    part = cmul(g[e], (q[0][e : e + 1], q[1][e : e + 1]))
                    re, im = re + part[0], im + part[1]
                ys.append((re, im))
        for m, (q, y) in enumerate(zip(done, ys)):
            level = row_dot(q, y)[0]
            levels[m : m + 1, :] = level
            factor = jnp.where(kept[...] > m, 1.0, 0.0) / jnp.sqrt(level)
            re, im = cmul(ph, q)
            re, im = re * factor, im * factor
            for t in range(count):
                lane = slice(t * LANES, (t + 1) * LANES)
                basis[t, 2 * m * blocks : (2 * m + 1) * blocks, :] = re[:, lane]
                basis[t, (2 * m + 1) * blocks : (2 * m + 2) * blocks, :] = im[:, lane]
        owned = energy.shape[1]
        bins = levels.shape[1]
        turned = pltpu.roll(levels[...], (bins - core[1] * owned) % bins, 1)
        energy[...] = turned[:MODES, :owned]

    make_basis()

    def project(t, carry):
        for copy in arrivals(t):
            copy.wait()
        where = []
        for n in range(parts):
            re, im = held[2 * n].at[t], held[2 * n + 1].at[t]
            where += [(re, im, n * LANES) for n in range(re.shape[0] // LANES)]
        for m in range(MODES):
            total = None
            for b, (re, im, base) in enumerate(where):
                u = (re[base : base + LANES, :], im[base : base + LANES, :])
                q = [basis[t, pl.ds((2 * m + n) * blocks + b, 1), :] for n in (0, 1)]
                part = cmul(u, q)
                total = part if b == 0 else (total[0] + part[0], total[1] + part[1])
            made[t, m, 0] = total[0]
            made[t, m, 1] = total[1]
        departure(t).start()
        return carry

    lax.fori_loop(0, steps, project, 0)
    for t in range(steps):
        departure(t).wait()


def finish(blocks, points, owned, core, mine, other, turn, kept, parts):
    square, half = mine.shape
    bins = 2 * half
    flat = [a for part in parts for a in part]
    kept = kept.reshape(1, bins)
    small = [mine, other, *turn, kept]
    steps = bins // LANES
    vmem = pl.BlockSpec(memory_space=pltpu.VMEM)
    return pl.pallas_call(
        lambda *refs: finish_kernel(blocks, points, len(parts), *refs),
        grid_spec=pltpu.PrefetchScalarGridSpec(
            num_scalar_prefetch=1,
            grid=(1,),
            in_specs=[vmem] * len(small) + [pl.BlockSpec(memory_space=pltpu.HBM)] * len(flat),
            out_specs=[vmem, pl.BlockSpec(memory_space=pltpu.HBM)],
            scratch_shapes=[
                pltpu.VMEM((steps, square, LANES), jnp.float32),
                pltpu.VMEM((steps, 2 * MODES * blocks, LANES), jnp.float32),
                pltpu.VMEM((8, bins), jnp.float32),
                pltpu.VMEM((steps, MODES, 2, LANES, LANES), jnp.float32),
                pltpu.SemaphoreType.DMA((steps, len(flat))),
                pltpu.SemaphoreType.DMA((steps,)),
            ]
            + [pltpu.VMEM((steps, a.shape[0], LANES), jnp.float32) for a in flat],
        ),
        out_shape=[
            jax.ShapeDtypeStruct((MODES, owned), jnp.float32),
            jax.ShapeDtypeStruct((MODES, 2, LANES, bins), jnp.float32),
        ],
        compiler_params=SMALL,
        cost_estimate=pl.CostEstimate(
            flops=16 * MODES * blocks * LANES * bins, bytes_accessed=6 * 2**20, transcendentals=0
        ),
    )(core, *small, *in_hbm(flat))


def gram_of(u, blocks):
    pairs = []
    for b, e in pair_list(blocks):
        pairs.append(jnp.sum(u[0][b] * u[0][e] + u[1][b] * u[1][e], axis=0))
        if e > b:
            pairs.append(jnp.sum(u[0][b] * u[1][e] - u[1][b] * u[0][e], axis=0))
    return jnp.stack(pairs, axis=0)


def plain(signal, offsets, pairing, modes_kept):
    rows, blocks, points = signal.shape
    ranks = lax.axis_size("freq")
    rank = lax.axis_index("freq")
    frames = rows * ranks
    bins = frames // 2
    own = points // ranks
    order = pairing.reshape(ranks, own // 2, 2).transpose(0, 2, 1).reshape(-1)
    packed = jnp.take(signal, order, axis=2).reshape(rows, blocks, ranks, own)
    packed = packed.transpose(2, 0, 1, 3)
    series = lax.all_to_all(packed, "freq", split_axis=0, concat_axis=0, tiled=True)
    series = series.reshape(frames, blocks * own)
    table = jnp.asarray(transform_table(frames))
    spectra = lax.dot_general(series, table, (((0,), (0,)), ((), ())), precision=precise)
    spectra = spectra.reshape(blocks, own, 2, bins)
    u = (spectra[:, :, 0], spectra[:, :, 1])
    sums = sum_over(gram_of(u, blocks), "freq") * (1.0 / points)
    g_re = [[None] * blocks for _ in range(blocks)]
    g_im = [[None] * blocks for _ in range(blocks)]
    at = 0
    for b in range(blocks):
        for e in range(b, blocks):
            g_re[b][e] = g_re[e][b] = sums[at]
            at += 1
            if e > b:
                g_im[b][e], g_im[e][b] = sums[at], -sums[at]
                at += 1
            else:
                g_im[b][b] = jnp.zeros_like(sums[0])
    g = (
        jnp.stack([jnp.stack(row) for row in g_re]),
        jnp.stack([jnp.stack(row) for row in g_im]),
    )
    turn = phase_table(offsets, bins, frames)
    both = cmul((turn[0][:, None], -turn[1][:, None]), (turn[0][None], turn[1][None]))
    basis, energy = leading_basis(cmul(both, g))
    live = jnp.arange(MODES, dtype=jnp.int32)[:, None] < modes_kept[None, :]
    factor = live.astype(jnp.float32) / jnp.sqrt(energy)
    modes = []
    for m in range(MODES):
        q = cmul(turn, basis[m])
        q = (q[0] * factor[m], q[1] * factor[m])
        re = jnp.sum(u[0] * q[0][:, None] - u[1] * q[1][:, None], axis=0)
        im = jnp.sum(u[0] * q[1][:, None] + u[1] * q[0][:, None], axis=0)
        modes.append(jnp.stack([re, im]))
    held = lax.dynamic_slice_in_dim(energy, rank * (bins // ranks), bins // ranks, axis=1)
    return held, jnp.stack(modes)


CHUNKS = (2, 6)


def swap_with(values, step):
    ranks = lax.axis_size("freq")
    return lax.ppermute(values, "freq", [(i, i ^ step) for i in range(ranks)])


def tiled(signal, offsets, pairing, modes_kept):
    rows, blocks, points = signal.shape
    ranks = lax.axis_size("freq")
    rank = lax.axis_index("freq")
    bins = rows * ranks // 2
    core = (rank & 1).reshape(1)
    turn = phase_table(offsets, bins, rows * ranks)
    tables = [jnp.asarray(t) for t in split_table(rows * ranks)]
    got, first = [], 0
    for count in CHUNKS:
        part = pack(signal, pairing, first, count)
        signal, part = lax.optimization_barrier((signal, part))
        got.append(lax.all_to_all(part, "freq", split_axis=0, concat_axis=0, tiled=True))
        first += count
    parts, gram = [], None
    for n, x in enumerate(got):
        final = n == len(got) - 1
        re, im, *grams = spectra(blocks, x.reshape(rows * ranks, -1), tables, core, parts, gram, final)
        parts.append((re, im))
        gram = grams[0]
    mine = gram + swap_with(grams[1], 1)
    step = 2
    while step < ranks:
        mine = mine + swap_with(mine, step)
        step *= 2
    other = swap_with(mine, 1)
    energy, modes = finish(
        blocks, points, bins // ranks, jnp.stack([rank & 1, rank]), mine, other, turn, modes_kept, parts
    )
    return energy, modes


def local(signal, offsets, pairing, modes_kept):
    rows, blocks, points = signal.shape
    ranks = lax.axis_size("freq")
    bins = rows * ranks // 2
    fits = points == ranks * LANES and rows % 16 == 0 and ranks >= GROUP and ranks & (ranks - 1) == 0
    fits = fits and bins % (2 * LANES) == 0 and blocks == sum(CHUNKS) == 8
    energy, modes = (tiled if fits else plain)(signal, offsets, pairing, modes_kept)
    modes = modes.reshape(MODES, 2, 2, points // ranks // 2, bins)
    return energy.T, modes.transpose(4, 0, 1, 2, 3)


def solution(mesh):
    placed = (P("freq", None, "groups"), P(), P("groups"), P())
    return jax.shard_map(
        local,
        mesh=mesh,
        in_specs=placed,
        out_specs=(P("freq", "groups"), P(None, None, None, None, ("groups", "freq"))),
        check_vma=False,
    )
```
